256 devices in a mesh: ka: 16 (over z_lo, x, core), vert: 16 (over y, z_hi).
Axes of the slice: x: 4, y: 4, z: 8 (z_hi: 4, z_lo: 2; z = z_hi * 2 + z_lo), core: 2. Of those that a mesh axis runs over, the one named last changes fastest.
Arguments:
- left_factor: bfloat16 [16, 1, 512, 176, 176], P('ka', None, 'vert'), may hold values from -0.4375 to 0.4375
- right_factor: bfloat16 [16, 1, 512, 176, 176], P('ka', None, 'vert'), may hold values from -0.109375 to 0.109375
- amplitudes: bfloat16 [16, 1, 176, 176], replicated, may hold values from -6 to 6
- kb_table: int32 [16], replicated, may hold values from 0 to 15, as said below
- pair_list: int32 [16, 2], replicated, may hold values from 0 to 31
- occ_energy: float32 [32], replicated, may hold values from -2 to -0.5
- vir_energy: float32 [16, 176], replicated, may hold values from 0.5 to 3
Outputs:
- doubles_update: float32 [16, 176, 16, 176], P('ka', 'vert')
The draws below stay inside these ranges and needn't reach their ends.
Inputs may be any that keep to these rules, and one draw needn't show every extreme that they name: kb_table[k] = (16 + kij - k) mod 16 for one pair momentum kij, so every sector appears once.
All inputs are finite; a program needn't handle non-finite values.
Results may differ from the reference program's by a relative error of at most 0.0029.
Values may be sent and summed in bfloat16 or wider, within the bound.
A program may use at most 192 MiB of HBM per device.

```python
import jax
import jax.numpy as jnp
from jax import lax

V = 176
NOCC = 32
NAUX = 512
KCW = 1
PAIRS = 16
K = 16


def draw_kb_table(key, part):
    key = jax.random.fold_in(key, 7)
    momentum = jax.random.randint(key, (), 0, K, dtype=jnp.int32)
    return (momentum + K - jnp.arange(K, dtype=jnp.int32)) % K


def with_ends(values, key, least, largest):
    place = [jax.random.randint(jax.random.fold_in(key, axis), (), 0, length) for axis, length in enumerate(values.shape)]
    longest = values.shape.index(max(values.shape))
    neighbour = place[:longest] + [(place[longest] + 1) % values.shape[longest]] + place[longest + 1:]
    return values.at[tuple(place)].set(least).at[tuple(neighbour)].set(largest)


def spiked(result, stream_key, source, target, shards_of, factor):
    owner, partner = [(jnp.arange(result.shape[position]) // (result.shape[position] // shards_of)).reshape([-1 if axis == position else 1 for axis in range(result.ndim)]) for position in (source, target)]
    chosen = jax.random.permutation(stream_key, shards_of)[partner]
    strong = (owner == chosen) | (owner == (partner + shards_of // 2) % shards_of)
    return jnp.where(strong, factor * result, result)


def block_scale(key, shape, shards, smallest, largest):
    factor_of = 1.0
    for dim, parts in shards:
        steps = jax.random.uniform(jax.random.fold_in(jax.random.fold_in(key, 6), dim), (parts,), jnp.float32, smallest / len(shards), largest / len(shards))
        factor_of = factor_of * jnp.repeat(jnp.exp(steps), shape[dim] // parts).reshape((-1,) + (1,) * (len(shape) - 1 - dim))
    return factor_of


def centred(stream_key, extent, deviation, reach, shards=(), held_as=jnp.bfloat16):
    entries = jax.random.normal(stream_key, extent, jnp.float32) * deviation
    if len(shards) > 0:
        entries = block_scale(stream_key, extent, shards, -0.22, 0.18) * entries
    return jnp.clip(entries, min=-reach, max=reach).astype(held_as)


def noise_with(own_key, shape, deviation, reach, pieces, heavy, held_as=jnp.bfloat16):
    drawn = deviation * jax.random.normal(own_key, shape, jnp.float32)
    if pieces:
        drawn = drawn * block_scale(own_key, shape, pieces, -0.22, 0.18)
    return jnp.clip(spiked(drawn, jax.random.fold_in(own_key, 3), *heavy), -reach, reach).astype(held_as)


def setup_inputs(seed: int = 0) -> dict:
    keys = jax.random.split(jax.random.key(seed), 8)
    return {
        "left_factor": centred(keys[0], (K, KCW, NAUX, V, V), V ** -0.5, 0.4375, ((0, 16), (2, 16))),
        "right_factor": noise_with(keys[1], (K, KCW, NAUX, V, V), (KCW * NAUX * V // 16) ** -0.5, 0.109375, ((0, 16), (2, 16)), (2, 3, 16, 2.0)),
        "amplitudes": centred(keys[2], (PAIRS, KCW, V, V), 1.0, 6.0),
        "kb_table": draw_kb_table(jax.random.fold_in(keys[7], 71), 0),
        "pair_list": with_ends(jax.random.randint(keys[4], (PAIRS, 2), 0, NOCC), jax.random.fold_in(keys[4], 1), 0, NOCC - 1).astype(jnp.int32),
        "occ_energy": jnp.clip(jax.random.uniform(keys[5], (NOCC,), jnp.float32, -2.0, -0.5), -2.0, -0.5),
        "vir_energy": jnp.clip(jax.random.uniform(keys[6], (K, V), jnp.float32, 0.5, 3.0), 0.5, 3.0),
    }


def reference(left_factor, right_factor, amplitudes, kb_table, pair_list, occ_energy, vir_energy):
    pair_amps = amplitudes.astype(jnp.float32)
    pair_energy = occ_energy[pair_list[:, 0]] + occ_energy[pair_list[:, 1]]

    def one_sector(sector):
        left_block = left_factor[sector].astype(jnp.float32)
        partner = kb_table[sector]
        right_block = right_factor[partner].astype(jnp.float32)

        def per_pair(amps_pair):
            half_step = jnp.einsum("slac,scd->slad", left_block, amps_pair).astype(jnp.bfloat16)
            return jnp.einsum("slad,slbd->ba", half_step.astype(jnp.float32), right_block)

        ladder = lax.map(per_pair, pair_amps)
        ladder = jnp.transpose(ladder, (1, 0, 2))
        denominator = pair_energy[None, :, None] - vir_energy[partner][:, None, None] - vir_energy[sector][None, None, :]
        return ladder / denominator

    return lax.map(one_sector, jnp.arange(K, dtype=jnp.int32))
```

```python
import jax
import jax.numpy as jnp
from jax import lax
from jax.experimental import pallas as pl
from jax.experimental.pallas import tpu as pltpu
from jax.sharding import PartitionSpec as P

MESH = pl.DeviceIdType.MESH
F32 = jnp.float32
BF16 = jnp.bfloat16

V = 176
AUX = 32
PAIRS = 16
SECTORS = 16
GROUP = 8
GROUPS = AUX // GROUP
GL = GROUP * V
KL = AUX * V
PA = PAIRS * V
HALF = PA // 2
QP = 4
R0, R1 = 8, 3
N0, N1 = 16 * R0, 16 * R1
CHIPS = 8
W1 = 384


def kernel(kb_ref, l_hbm, r_hbm, t_hbm, o_ref,
           l_v, r_v, t_v, t_cat, send0, send1, mid_a, mid_b, mid_c, out0, out1, recv0, recv1, h, acc0, acc1,
           full0, ysend0, yrecv0, sum0, zsend0, zrecv0,
           full1, ysend1, yrecv1, zsend1, zrecv1,
           in_sem, ps_sem, pr_sem, qs_sem, qr_sem, ys_sem, yr_sem, zs_sem, zr_sem):
    me = lax.axis_index("ka")
    vert = lax.axis_index("vert")
    chip, core = me // 2, me % 2
    y, z = vert // 4, vert % 4
    y_peers = [(me, lax.rem(y + s, 4) * 4 + z) for s in (1, 2, 3)]
    z_peers = [(me, y * 4 + lax.rem(z + s, 4)) for s in (1, 2, 3)]

    def r_in(g):
        return pltpu.make_async_copy(r_hbm.at[pl.ds(g * GROUP, GROUP)], r_v.at[pl.ds(g * GROUP, GROUP)], in_sem.at[g])

    def l_in(g):
        rows = pl.ds(pl.multiple_of(g * GL, 16), GL)
        return pltpu.make_async_copy(l_hbm.at[rows], l_v.at[rows], in_sem.at[GROUPS + g])

    t_in = pltpu.make_async_copy(t_hbm, t_v, in_sem.at[2 * GROUPS])
    for g in range(GROUPS):
        r_in(g).start()
    t_in.start()
    for g in range(GROUPS):
        l_in(g).start()

    barrier = pltpu.get_barrier_semaphore()
    for peer in y_peers + z_peers:
        pl.semaphore_signal(barrier, inc=1, device_id=peer, device_id_type=MESH)

    @pl.loop(1, SECTORS)
    def _(s):
        pl.semaphore_signal(barrier, inc=1, device_id=(lax.rem(me + s, SECTORS), vert), device_id_type=MESH)

    mids = (mid_a, mid_b, mid_c)

    row = lax.broadcasted_iota(jnp.int32, (V, V), 0)
    col = lax.broadcasted_iota(jnp.int32, (V, V), 1)
    late = row - N0
    third = lax.shift_right_logical(late * 21846, 16)
    source = jnp.where(row < N0, 11 * lax.shift_right_logical(row, 3) + (row & 7), 11 * third + R0 + (late - 3 * third))
    order = (col == source).astype(F32).astype(BF16)

    for half in range(2):
        send1[half, :, 2 * GL:] = jnp.zeros((N1, W1 * CHIPS - 2 * GL), BF16)
    pl.semaphore_wait(barrier, SECTORS - 1 + 6)

    def hop(src, dst, send_sem, recv_sem, target, far):
        if far:
            return pltpu.make_async_remote_copy(
                src_ref=src, dst_ref=dst, send_sem=send_sem, recv_sem=recv_sem,
                device_id=(target, vert), device_id_type=MESH,
            )
        return pltpu.make_async_copy(src, dst, recv_sem)

    def first(unit, s, far):
        j = lax.rem(chip + s, CHIPS)
        if unit < GROUPS:
            src = send0.at[pl.ds(pl.multiple_of(16 * j, 16), 16), pl.ds(unit * GL, GL)]
            dst = mids[unit // 2].at[me]
            which = unit // 2
        else:
            src = send1.at[unit - GROUPS, :, pl.ds(pl.multiple_of(W1 * j, 128), W1)]
            dst = mids[2].at[me]
            which = 2
        return hop(src, dst, ps_sem.at[unit, s], pr_sem.at[which], 2 * j + unit % 2, far)

    def second(which, s, t, far):
        j = lax.rem(chip + s, CHIPS)
        k = 2 * j + t
        if which < 2:
            src = out0.at[which, k]
            g = 2 * which + core
            dst = recv0.at[pl.ds(pl.multiple_of(16 * chip, 16), 16), pl.ds(pl.multiple_of(g * GL, 128), GL)]
        else:
            src = out1.at[k]
            g = GROUPS + core
            dst = recv1.at[core, :, pl.ds(pl.multiple_of(W1 * chip, 128), W1)]
        return hop(src, dst, qs_sem.at[which, 2 * s + t], qr_sem.at[g], k, far)

    def start_first(unit):
        @pl.when(core == unit % 2)
        def _():
            first(unit, 0, False).start()

        @pl.when(core != unit % 2)
        def _():
            first(unit, 0, True).start()

        for s in range(1, CHIPS):
            first(unit, s, True).start()

    def start_second(which):
        mid, out = mids[which], out0.at[which] if which < 2 else out1
        pltpu.make_async_copy(mid, mid, pr_sem.at[which]).wait()

        @pl.loop(0, SECTORS)
        def _(k):
            out[k] = mid[kb_ref[k]]

        for s in range(1, CHIPS):
            for t in range(2):
                second(which, s, t, True).start()
        for t in range(2):
            @pl.when(core == t)
            def _():
                second(which, 0, t, False).start()

            @pl.when(core != t)
            def _():
                second(which, 0, t, True).start()

    for g in range(GROUPS):
        r_in(g).wait()
        parts = [jnp.dot(order, r_v[g * GROUP + i], preferred_element_type=F32).astype(BF16) for i in range(GROUP)]
        packed = jnp.concatenate(parts, axis=1)
        send0[:, g * GL:(g + 1) * GL] = packed[:N0]
        send1[g // 2, :, (g % 2) * GL:(g % 2 + 1) * GL] = packed[N0:]
        start_first(g)
    for half in range(2):
        start_first(GROUPS + half)

    t_in.wait()
    for q in range(PAIRS // QP):
        t_cat[q] = jnp.concatenate([t_v[q * QP + i] for i in range(QP)], axis=1)

    @pl.loop(0, GROUPS)
    def _(g):
        l_in(g).wait()

        @pl.loop(0, PAIRS // QP)
        def _(q):
            amps = t_cat[q]
            outs = []
            for i in range(GROUP):
                rows = pl.ds(pl.multiple_of(g * GL + i * V, 16), V)
                outs.append(jnp.dot(l_v[rows, :], amps, preferred_element_type=F32).astype(BF16))
            for i in range(QP):
                rows = pl.ds(pl.multiple_of(q * QP * V + i * V, 16), V)
                h[rows, pl.ds(pl.multiple_of(g * GL, 128), GL)] = jnp.concatenate(
                    [o[:, i * V:(i + 1) * V] for o in outs], axis=1
                )

        @pl.when(g == GROUPS - 2)
        def _():
            start_second(0)

    start_second(1)
    start_second(2)

    def add(acc, right, g):
        lanes = pl.ds(pl.multiple_of(g * GL, 128), GL)

        @pl.loop(0, 4)
        def _(m):
            rows = pl.ds(pl.multiple_of(m * (PA // 4), 16), PA // 4)
            acc[rows, :] += lax.dot_general(
                h[rows, lanes], right[...], (((1,), (1,)), ((), ())), preferred_element_type=F32
            )

    def add0(g):
        part = recv0.at[:, pl.ds(pl.multiple_of(g * GL, 128), GL)]
        pltpu.make_async_copy(part, part, qr_sem.at[g]).wait()
        add(acc0, part, g)

    def add1(g):
        half = g // 2

        @pl.when(lax.rem(g, 2) == 0)
        def _():
            pltpu.make_async_copy(recv1.at[half], recv1.at[half], qr_sem.at[GROUPS + half]).wait()

        add(acc1, recv1.at[half, :, pl.ds(pl.multiple_of(lax.rem(g, 2) * GL, 128), GL)], g)

    acc0[...] = jnp.zeros_like(acc0)
    acc1[...] = jnp.zeros_like(acc1)
    full1[...] = jnp.zeros_like(full1)
    zsend1[...] = jnp.zeros_like(zsend1)

    @pl.loop(0, GROUPS)
    def _(g):
        add0(g)

    def y_copy(chunk, s):
        src, dst = (ysend0, yrecv0) if chunk == 0 else (ysend1, yrecv1)
        return pltpu.make_async_remote_copy(
            src_ref=src.at[lax.rem(y + s, 4)], dst_ref=dst.at[s - 1],
            send_sem=ys_sem.at[chunk, s - 1], recv_sem=yr_sem.at[chunk, s - 1],
            device_id=y_peers[s - 1], device_id_type=MESH,
        )

    def z_copy(chunk, s):
        src, dst = (zsend0, zrecv0) if chunk == 0 else (zsend1, zrecv1)
        return pltpu.make_async_remote_copy(
            src_ref=src.at[lax.rem(z + s, 4)], dst_ref=dst.at[s - 1],
            send_sem=zs_sem.at[chunk, s - 1], recv_sem=zr_sem.at[chunk, s - 1],
            device_id=z_peers[s - 1], device_id_type=MESH,
        )

    @pl.loop(0, PA // 128)
    def _(m):
        at = pl.ds(pl.multiple_of(m * 128, 128), 128)
        turned = acc0[at, :].T
        full0[:, at] = turned
        for j in range(4):
            ysend0[j, :, at] = turned[32 * j:32 * (j + 1)].astype(BF16)

    for s in (1, 2, 3):
        y_copy(0, s).start()

    @pl.loop(0, GROUPS - 1)
    def _(g):
        add1(g)

    for s in (1, 2, 3):
        y_copy(0, s).wait()
    total = full0[pl.ds(pl.multiple_of(32 * y, 8), 32), :]
    for s in range(3):
        total = total + yrecv0[s].astype(F32)
    sum0[...] = total
    for j in range(4):
        part = sum0[8 * j:8 * (j + 1), :]
        zsend0[j] = jnp.concatenate([part[:, :HALF], part[:, HALF:]], axis=0).astype(BF16)
    for s in (1, 2, 3):
        z_copy(0, s).start()

    add1(jnp.int32(GROUPS - 1))

    @pl.loop(0, PA // 128)
    def _(m):
        at = pl.ds(pl.multiple_of(m * 128, 128), 128)
        turned = acc1[at, :].T
        for j in range(4):
            full1[j, 0:12, at] = turned[12 * j:12 * (j + 1)]
    for j in range(4):
        ysend1[j] = full1[j].astype(BF16)
    for s in (1, 2, 3):
        y_copy(1, s).start()

    for s in (1, 2, 3):
        z_copy(0, s).wait()
    own = sum0[pl.ds(pl.multiple_of(8 * z, 8), 8), :]
    low, high = own[:, :HALF], own[:, HALF:]
    for s in range(3):
        got = zrecv0[s].astype(F32)
        low, high = low + got[0:8], high + got[8:16]
    o_ref[0:8, :HALF] = low
    o_ref[0:8, HALF:] = high

    for s in (1, 2, 3):
        y_copy(1, s).wait()
    rest = full1[y]
    for s in range(3):
        rest = rest + yrecv1[s].astype(F32)
    for j in range(4):
        zsend1[j, 0:3, :] = rest[3 * j:3 * j + 3, :HALF]
        zsend1[j, 4:7, :] = rest[3 * j:3 * j + 3, HALF:]
    for s in (1, 2, 3):
        z_copy(1, s).start()
    for s in (1, 2, 3):
        z_copy(1, s).wait()
    last = zsend1[z]
    for s in range(3):
        last = last + zrecv1[s]
    o_ref[8:16, :HALF] = last
    o_ref[8:12, HALF:] = last[4:8]
    o_ref[12:16, HALF:] = last[4:8]

    for unit in range(GROUPS + 2):
        @pl.when(core != unit % 2)
        def _():
            first(unit, 0, True).wait_send()

        for s in range(1, CHIPS):
            first(unit, s, True).wait_send()
    for which in range(3):
        for t in range(2):
            @pl.when(core != t)
            def _():
                second(which, 0, t, True).wait_send()

            for s in range(1, CHIPS):
                second(which, s, t, True).wait_send()


def ladder_of(kb_table, left, right, amps):
    any_space = pl.BlockSpec(memory_space=pl.ANY)
    vmem = pltpu.VMEM
    return pl.pallas_call(
        kernel,
        out_shape=jax.ShapeDtypeStruct((16, PA), F32),
        in_specs=[pl.BlockSpec(memory_space=pltpu.SMEM)] + [any_space] * 3,
        out_specs=pl.BlockSpec(memory_space=pltpu.VMEM),
        scratch_shapes=[
            vmem((KL, V), BF16), vmem((AUX, V, V), BF16), vmem((PAIRS, V, V), BF16),
            vmem((PAIRS // QP, V, QP * V), BF16),
            vmem((N0, KL), BF16), vmem((2, N1, W1 * CHIPS), BF16),
            vmem((SECTORS, 16, GL), BF16), vmem((SECTORS, 16, GL), BF16), vmem((SECTORS, N1, W1), BF16),
            vmem((2, SECTORS, 16, GL), BF16), vmem((SECTORS, N1, W1), BF16),
            vmem((N0, KL), BF16), vmem((2, N1, W1 * CHIPS), BF16), vmem((PA, KL), BF16),
            vmem((PA, N0), F32), vmem((PA, N1), F32),
            vmem((N0, PA), F32), vmem((4, 32, PA), BF16), vmem((3, 32, PA), BF16),
            vmem((32, PA), F32), vmem((4, 16, HALF), BF16), vmem((3, 16, HALF), BF16),
            vmem((4, 16, PA), F32), vmem((4, 16, PA), BF16), vmem((3, 16, PA), BF16),
            vmem((4, 8, HALF), F32), vmem((3, 8, HALF), F32),
            pltpu.SemaphoreType.DMA((2 * GROUPS + 1,)),
            pltpu.SemaphoreType.DMA((GROUPS + 2, CHIPS)), pltpu.SemaphoreType.DMA((3,)),
            pltpu.SemaphoreType.DMA((3, SECTORS)), pltpu.SemaphoreType.DMA((GROUPS + 2,)),
            pltpu.SemaphoreType.DMA((2, 3)), pltpu.SemaphoreType.DMA((2, 3)),
            pltpu.SemaphoreType.DMA((2, 3)), pltpu.SemaphoreType.DMA((2, 3)),
        ],
        compiler_params=pltpu.CompilerParams(
            collective_id=0, has_side_effects=True, vmem_limit_bytes=60 * 2**20
        ),
    )(kb_table, left, right, amps)


def on_device(left_factor, right_factor, amplitudes, kb_table, pair_list, occ_energy, vir_energy):
    sector = lax.axis_index("ka")
    sectors = lax.axis_size("ka")
    column = lax.axis_index("vert")
    b_rows = V // lax.axis_size("vert")
    partner = kb_table[sector]
    left = left_factor.reshape(KL, V)
    right = right_factor.reshape(AUX, V, V)
    amps = amplitudes.reshape(PAIRS, V, V)
    ladder = ladder_of(kb_table, left, right, amps)[:b_rows].reshape(b_rows, PAIRS, V)
    occ_ids = jnp.arange(occ_energy.shape[0], dtype=jnp.int32)
    onehot = pair_list[:, :, None] == occ_ids[None, None, :]
    pair_energy = jnp.sum(jnp.where(onehot, occ_energy[None, None, :], 0.0), axis=(1, 2))
    sector_ids = jnp.arange(sectors, dtype=jnp.int32)
    partner_vir = jnp.sum(jnp.where((sector_ids == partner)[:, None], vir_energy, 0.0), axis=0)
    own_vir = jnp.sum(jnp.where((sector_ids == sector)[:, None], vir_energy, 0.0), axis=0)
    b_energy = lax.dynamic_slice_in_dim(partner_vir, column * b_rows, b_rows, 0)
    denominator = pair_energy[None, :, None] - b_energy[:, None, None] - own_vir[None, None, :]
    return (ladder / denominator)[None]


def solution(mesh):
    placed = (
        P("ka", None, "vert", None, None),
        P("ka", None, "vert", None, None),
        P(),
        P(),
        P(),
        P(),
        P(),
    )
    return jax.shard_map(
        on_device,
        mesh=mesh,
        in_specs=placed,
        out_specs=P("ka", "vert", None, None),
        check_vma=False,
    )
```

```python
import jax
import jax.numpy as jnp
from jax import lax
from jax.experimental import pallas as pl
from jax.experimental.pallas import tpu as pltpu
from jax.sharding import PartitionSpec as P

MESH = pl.DeviceIdType.MESH
F32 = jnp.float32
BF16 = jnp.bfloat16

V = 176
AUX = 32
PAIRS = 16
SECTORS = 16
GROUP = 8
GROUPS = AUX // GROUP
GL = GROUP * V
KL = AUX * V
PA = PAIRS * V
HALF = PA // 2
QP = 4
R0, R1 = 8, 3
N0, N1 = 16 * R0, 16 * R1
CHIPS = 8
W2 = 768
W1 = 384


def kernel(kb_ref, pair_ref, occ_ref, vir_ref, own_vir_ref, l_hbm, r_hbm, t_hbm, o_ref,
           l_v, r_v, t_v, t_cat, send0, send1, mid_a, mid_b, mid_c, out0, out1, recv0, recv1, h, acc0, acc1, den,
           full0, ysend0, yrecv0, sum0, zsend0, zrecv0,
           full1, ysend1, yrecv1, zsend1, zrecv1,
           in_sem, ps_sem, pr_sem, qs_sem, qr_sem, ys_sem, yr_sem, zs_sem, zr_sem):
    me = lax.axis_index("ka")
    vert = lax.axis_index("vert")
    chip, core = me // 2, me % 2
    y, z = vert // 4, vert % 4
    y_peers = [(me, lax.rem(y + s, 4) * 4 + z) for s in (1, 2, 3)]
    z_peers = [(me, y * 4 + lax.rem(z + s, 4)) for s in (1, 2, 3)]

    def r_in(g):
        return pltpu.make_async_copy(r_hbm.at[pl.ds(g * GROUP, GROUP)], r_v.at[pl.ds(g * GROUP, GROUP)], in_sem.at[g])

    def l_in(g):
        rows = pl.ds(pl.multiple_of(g * GL, 16), GL)
        return pltpu.make_async_copy(l_hbm.at[rows], l_v.at[rows], in_sem.at[GROUPS + g])

    t_in = pltpu.make_async_copy(t_hbm, t_v, in_sem.at[2 * GROUPS])
    for g in range(GROUPS):
        r_in(g).start()
    t_in.start()
    for g in range(GROUPS):
        l_in(g).start()

    barrier = pltpu.get_barrier_semaphore()
    for peer in y_peers + z_peers:
        pl.semaphore_signal(barrier, inc=1, device_id=peer, device_id_type=MESH)

    @pl.loop(1, SECTORS)
    def _(s):
        pl.semaphore_signal(barrier, inc=1, device_id=(lax.rem(me + s, SECTORS), vert), device_id_type=MESH)

    mids = (mid_a, mid_b, mid_c)

    row = lax.broadcasted_iota(jnp.int32, (V, V), 0)
    col = lax.broadcasted_iota(jnp.int32, (V, V), 1)
    late = row - N0
    third = lax.shift_right_logical(late * 21846, 16)
    source = jnp.where(row < N0, 11 * lax.shift_right_logical(row, 3) + (row & 7), 11 * third + R0 + (late - 3 * third))
    order = (col == source).astype(F32).astype(BF16)

    for half in range(2):
        send1[half, :, 2 * GL:] = jnp.zeros((N1, W1 * CHIPS - 2 * GL), BF16)

    def hop(src, dst, send_sem, recv_sem, target, far):
        if far:
            return pltpu.make_async_remote_copy(
                src_ref=src, dst_ref=dst, send_sem=send_sem, recv_sem=recv_sem,
                device_id=(target, vert), device_id_type=MESH,
            )
        return pltpu.make_async_copy(src, dst, recv_sem)

    def first(unit, s, far):
        j = lax.rem(chip + s, CHIPS)
        if unit < GROUPS:
            src = send0.at[pl.ds(pl.multiple_of(16 * j, 16), 16), pl.ds(unit * GL, GL)]
            dst = mids[unit // 2].at[me]
            which = unit // 2
        else:
            src = send1.at[unit - GROUPS, :, pl.ds(pl.multiple_of(W1 * j, 128), W1)]
            dst = mids[2].at[me]
            which = 2
        return hop(src, dst, ps_sem.at[unit, s], pr_sem.at[which], 2 * j + unit % 2, far)

    def second(which, s, t, far):
        j = lax.rem(chip + s, CHIPS)
        k = 2 * j + t
        if which < 2:
            src = out0.at[which, k]
            g = 2 * which + core
            dst = recv0.at[pl.ds(pl.multiple_of(16 * chip, 16), 16), pl.ds(pl.multiple_of(g * GL, 128), GL)]
        else:
            src = out1.at[k]
            g = GROUPS + core
            dst = recv1.at[core, :, pl.ds(pl.multiple_of(W1 * chip, 128), W1)]
        return hop(src, dst, qs_sem.at[which, 2 * s + t], qr_sem.at[g], k, far)

    def start_first(unit):
        @pl.when(core == unit % 2)
        def _():
            first(unit, 0, False).start()

        @pl.when(core != unit % 2)
        def _():
            first(unit, 0, True).start()

        for s in range(1, CHIPS):
            first(unit, s, True).start()

    def start_second(which):
        mid, out = mids[which], out0.at[which] if which < 2 else out1
        pltpu.make_async_copy(mid, mid, pr_sem.at[which]).wait()

        @pl.loop(0, SECTORS)
        def _(k):
            out[k] = mid[kb_ref[k]]

        for s in range(1, CHIPS):
            for t in range(2):
                second(which, s, t, True).start()
        for t in range(2):
            @pl.when(core == t)
            def _():
                second(which, 0, t, False).start()

            @pl.when(core != t)
            def _():
                second(which, 0, t, True).start()

    for g in range(GROUPS):
        r_in(g).wait()
        parts = [jnp.dot(order, r_v[g * GROUP + i], preferred_element_type=F32).astype(BF16) for i in range(GROUP)]
        packed = jnp.concatenate(parts, axis=1)
        send0[:, g * GL:(g + 1) * GL] = packed[:N0]
        send1[g // 2, :, (g % 2) * GL:(g % 2 + 1) * GL] = packed[N0:]
        if g == 0:
            pl.semaphore_wait(barrier, SECTORS - 1 + 6)
        start_first(g)
    for half in range(2):
        start_first(GROUPS + half)

    pair_row = jnp.concatenate(
        [jnp.full((1, V), occ_ref[pair_ref[p, 0]] + occ_ref[pair_ref[p, 1]], F32) for p in range(PAIRS)], axis=1
    )
    own_vir = own_vir_ref[pl.ds(me, 1), :]
    own_row = jnp.concatenate([own_vir] * PAIRS, axis=1)
    for r in range(R0 + R1):
        den[r:r + 1, :] = (pair_row - vir_ref[kb_ref[me], (R0 + R1) * vert + r]) - own_row

    t_in.wait()
    for q in range(PAIRS // QP):
        t_cat[q] = jnp.concatenate([t_v[q * QP + i] for i in range(QP)], axis=1)

    @pl.loop(0, GROUPS)
    def _(g):
        l_in(g).wait()

        @pl.loop(0, PAIRS // QP)
        def _(q):
            amps = t_cat[q]
            outs = []
            for i in range(GROUP):
                rows = pl.ds(pl.multiple_of(g * GL + i * V, 16), V)
                outs.append(jnp.dot(l_v[rows, :], amps, preferred_element_type=F32).astype(BF16))
            for i in range(QP):
                rows = pl.ds(pl.multiple_of(q * QP * V + i * V, 16), V)
                h[rows, pl.ds(pl.multiple_of(g * GL, 128), GL)] = jnp.concatenate(
                    [o[:, i * V:(i + 1) * V] for o in outs], axis=1
                )

        @pl.when(g == GROUPS // 2 - 1)
        def _():
            start_second(0)

    start_second(1)

    def add(acc, right, half):
        lanes = pl.ds(half * 2 * GL, 2 * GL)

        @pl.loop(0, 4)
        def _(m):
            rows = pl.ds(pl.multiple_of(m * (PA // 4), 16), PA // 4)
            term = lax.dot_general(
                h[rows, lanes], right[...], (((1,), (1,)), ((), ())), preferred_element_type=F32
            )
            acc[rows, :] = term if half == 0 else acc[rows, :] + term

    def add0(half):
        for g in (2 * half, 2 * half + 1):
            part = recv0.at[:, pl.ds(g * GL, GL)]
            pltpu.make_async_copy(part, part, qr_sem.at[g]).wait()
        add(acc0, recv0.at[:, pl.ds(half * 2 * GL, 2 * GL)], half)

    def add1(half):
        pltpu.make_async_copy(recv1.at[half], recv1.at[half], qr_sem.at[GROUPS + half]).wait()
        add(acc1, recv1.at[half, :, pl.ds(0, 2 * GL)], half)

    full1[...] = jnp.zeros_like(full1)
    zsend1[...] = jnp.zeros_like(zsend1)
    add0(0)
    start_second(2)
    add0(1)

    def y_copy(part, s):
        src, dst = (ysend0, yrecv0) if part == 0 else (ysend1.at[part - 1], yrecv1.at[part - 1])
        return pltpu.make_async_remote_copy(
            src_ref=src.at[lax.rem(y + s, 4)], dst_ref=dst.at[s - 1],
            send_sem=ys_sem.at[part, s - 1], recv_sem=yr_sem.at[part, s - 1],
            device_id=y_peers[s - 1], device_id_type=MESH,
        )

    def z_copy(part, s):
        src, dst = (zsend0, zrecv0) if part == 0 else (zsend1.at[part - 1], zrecv1.at[part - 1])
        return pltpu.make_async_remote_copy(
            src_ref=src.at[lax.rem(z + s, 4)], dst_ref=dst.at[s - 1],
            send_sem=zs_sem.at[part, s - 1], recv_sem=zr_sem.at[part, s - 1],
            device_id=z_peers[s - 1], device_id_type=MESH,
        )

    @pl.loop(0, PA // 128)
    def _(m):
        at = pl.ds(pl.multiple_of(m * 128, 128), 128)
        turned = acc0[at, :].T
        full0[:, at] = turned
        for j in range(4):
            ysend0[j, :, at] = turned[32 * j:32 * (j + 1)].astype(BF16)

    for s in (1, 2, 3):
        y_copy(0, s).start()

    add1(0)

    for s in (1, 2, 3):
        y_copy(0, s).wait()
    total = full0[pl.ds(pl.multiple_of(32 * y, 8), 32), :]
    for s in range(3):
        total = total + yrecv0[s].astype(F32)
    sum0[...] = total
    for j in range(4):
        part = sum0[8 * j:8 * (j + 1), :]
        zsend0[j] = jnp.concatenate([part[:, :HALF], part[:, HALF:]], axis=0).astype(BF16)
    for s in (1, 2, 3):
        z_copy(0, s).start()

    add1(1)

    for part in (1, 2):
        @pl.loop(0, HALF // 128)
        def _(m):
            at = pl.ds(pl.multiple_of(m * 128, 128), 128)
            turned = acc1[pl.ds(pl.multiple_of((part - 1) * HALF + m * 128, 128), 128), :].T
            for j in range(4):
                full1[part - 1, j, 0:12, at] = turned[12 * j:12 * (j + 1)]

        ysend1[part - 1] = full1[part - 1].astype(BF16)
        for s in (1, 2, 3):
            y_copy(part, s).start()

    for s in (1, 2, 3):
        z_copy(0, s).wait()
    own = sum0[pl.ds(pl.multiple_of(8 * z, 8), 8), :]
    low, high = own[:, :HALF], own[:, HALF:]
    for s in range(3):
        got = zrecv0[s].astype(F32)
        low, high = low + got[0:8], high + got[8:16]
    o_ref[0:8, :HALF] = low / den[0:8, :HALF]
    o_ref[0:8, HALF:] = high / den[0:8, HALF:]

    for part in (1, 2):
        for s in (1, 2, 3):
            y_copy(part, s).wait()
        rest = full1[part - 1, y]
        for s in range(3):
            rest = rest + yrecv1[part - 1, s].astype(F32)
        for j in range(4):
            zsend1[part - 1, j, 0:3, :] = rest[3 * j:3 * j + 3, :W2]
            zsend1[part - 1, j, 4:7, :HALF - W2] = rest[3 * j:3 * j + 3, W2:]
        for s in (1, 2, 3):
            z_copy(part, s).start()
    for part in (1, 2):
        for s in (1, 2, 3):
            z_copy(part, s).wait()
        last = zsend1[part - 1, z]
        for s in range(3):
            last = last + zrecv1[part - 1, s]
        at = (part - 1) * HALF
        o_ref[8:11, at:at + W2] = last[0:3] / den[8:11, at:at + W2]
        o_ref[8:11, at + W2:at + HALF] = last[4:7, :HALF - W2] / den[8:11, at + W2:at + HALF]

    for unit in range(GROUPS + 2):
        @pl.when(core != unit % 2)
        def _():
            first(unit, 0, True).wait_send()

        for s in range(1, CHIPS):
            first(unit, s, True).wait_send()
    for which in range(3):
        for t in range(2):
            @pl.when(core != t)
            def _():
                second(which, 0, t, True).wait_send()

            for s in range(1, CHIPS):
                second(which, s, t, True).wait_send()


def update_of(kb_table, pair_list, occ_energy, vir_energy, left, right, amps):
    any_space = pl.BlockSpec(memory_space=pl.ANY)
    smem = pl.BlockSpec(memory_space=pltpu.SMEM)
    vmem = pltpu.VMEM
    return pl.pallas_call(
        kernel,
        out_shape=jax.ShapeDtypeStruct((R0 + R1, PA), F32),
        in_specs=[smem] * 4 + [pl.BlockSpec(memory_space=pltpu.VMEM)] + [any_space] * 3,
        out_specs=pl.BlockSpec(memory_space=pltpu.VMEM),
        scratch_shapes=[
            vmem((KL, V), BF16), vmem((AUX, V, V), BF16), vmem((PAIRS, V, V), BF16),
            vmem((PAIRS // QP, V, QP * V), BF16),
            vmem((N0, KL), BF16), vmem((2, N1, W1 * CHIPS), BF16),
            vmem((SECTORS, 16, GL), BF16), vmem((SECTORS, 16, GL), BF16), vmem((SECTORS, N1, W1), BF16),
            vmem((2, SECTORS, 16, GL), BF16), vmem((SECTORS, N1, W1), BF16),
            vmem((N0, KL), BF16), vmem((2, N1, W1 * CHIPS), BF16), vmem((PA, KL), BF16),
            vmem((PA, N0), F32), vmem((PA, N1), F32), vmem((16, PA), F32),
            vmem((N0, PA), F32), vmem((4, 32, PA), BF16), vmem((3, 32, PA), BF16),
            vmem((32, PA), F32), vmem((4, 16, HALF), BF16), vmem((3, 16, HALF), BF16),
            vmem((2, 4, 16, HALF), F32), vmem((2, 4, 16, HALF), BF16), vmem((2, 3, 16, HALF), BF16),
            vmem((2, 4, 8, W2), F32), vmem((2, 3, 8, W2), F32),
            pltpu.SemaphoreType.DMA((2 * GROUPS + 1,)),
            pltpu.SemaphoreType.DMA((GROUPS + 2, CHIPS)), pltpu.SemaphoreType.DMA((3,)),
            pltpu.SemaphoreType.DMA((3, SECTORS)), pltpu.SemaphoreType.DMA((GROUPS + 2,)),
            pltpu.SemaphoreType.DMA((3, 3)), pltpu.SemaphoreType.DMA((3, 3)),
            pltpu.SemaphoreType.DMA((3, 3)), pltpu.SemaphoreType.DMA((3, 3)),
        ],
        compiler_params=pltpu.CompilerParams(
            collective_id=0, has_side_effects=True, vmem_limit_bytes=60 * 2**20
        ),
    )(kb_table, pair_list, occ_energy, vir_energy, vir_energy, left, right, amps)


def on_device(left_factor, right_factor, amplitudes, kb_table, pair_list, occ_energy, vir_energy):
    left = left_factor.reshape(KL, V)
    right = right_factor.reshape(AUX, V, V)
    amps = amplitudes.reshape(PAIRS, V, V)
    update = update_of(kb_table, pair_list, occ_energy, vir_energy, left, right, amps)
    return update.reshape(1, R0 + R1, PAIRS, V)


def solution(mesh):
    placed = (
        P("ka", None, "vert", None, None),
        P("ka", None, "vert", None, None),
        P(),
        P(),
        P(),
        P(),
        P(),
    )
    return jax.shard_map(
        on_device,
        mesh=mesh,
        in_specs=placed,
        out_specs=P("ka", "vert", None, None),
        check_vma=False,
    )
```

```python
import jax
import jax.numpy as jnp
from jax import lax
from jax.experimental import pallas as pl
from jax.experimental.pallas import tpu as pltpu
from jax.sharding import PartitionSpec as P

MESH = pl.DeviceIdType.MESH
F32 = jnp.float32
BF16 = jnp.bfloat16

V = 176
AUX = 32
PAIRS = 16
SECTORS = 16
GROUP = 8
GROUPS = AUX // GROUP
GL = GROUP * V
KL = AUX * V
PA = PAIRS * V
HALF = PA // 2
ROWS = PA // 4
QP = 4
R0, R1 = 8, 3
N0, N1 = 16 * R0, 16 * R1
CHIPS = 8
W2 = 768
W1 = 384


def kernel(kb_ref, pair_ref, occ_ref, vir_ref, own_vir_ref, l_hbm, r_hbm, t_hbm, o_ref,
           l_v, r_v, t_v, t_cat, send0, send1, mid_a, mid_b, mid_c, out0, out1, recv0, recv1, h, acc0, acc1, den,
           full0, ysend0, yrecv0, sum0, zsend0, zrecv0,
           full1, ysend1, yrecv1, zsend1, zrecv1,
           in_sem, ps_sem, pr_sem, qs_sem, qr_sem, ys_sem, yr_sem, zs_sem, zr_sem):
    me = lax.axis_index("ka")
    vert = lax.axis_index("vert")
    chip, core = me // 2, me % 2
    y, z = vert // 4, vert % 4
    y_peers = [(me, lax.rem(y + s, 4) * 4 + z) for s in (1, 2, 3)]
    z_peers = [(me, y * 4 + lax.rem(z + s, 4)) for s in (1, 2, 3)]

    barrier = pltpu.get_barrier_semaphore()
    for peer in y_peers + z_peers:
        pl.semaphore_signal(barrier, inc=1, device_id=peer, device_id_type=MESH)

    @pl.loop(1, SECTORS)
    def _(s):
        pl.semaphore_signal(barrier, inc=1, device_id=(lax.rem(me + s, SECTORS), vert), device_id_type=MESH)

    def r_in(g):
        return pltpu.make_async_copy(r_hbm.at[pl.ds(g * GROUP, GROUP)], r_v.at[pl.ds(g * GROUP, GROUP)], in_sem.at[g])

    def l_in(g):
        rows = pl.ds(pl.multiple_of(g * GL, 16), GL)
        return pltpu.make_async_copy(l_hbm.at[rows], l_v.at[rows], in_sem.at[GROUPS + g])

    t_in = pltpu.make_async_copy(t_hbm, t_v, in_sem.at[2 * GROUPS])
    for g in range(GROUPS):
        r_in(g).start()
    t_in.start()
    for g in range(GROUPS):
        l_in(g).start()

    mids = (mid_a, mid_b, mid_c)

    row = lax.broadcasted_iota(jnp.int32, (V, V), 0)
    col = lax.broadcasted_iota(jnp.int32, (V, V), 1)
    late = row - N0
    third = lax.shift_right_logical(late * 21846, 16)
    source = jnp.where(row < N0, 11 * lax.shift_right_logical(row, 3) + (row & 7), 11 * third + R0 + (late - 3 * third))
    order = (col == source).astype(F32).astype(BF16)

    for half in range(2):
        send1[half, :, 2 * GL:] = jnp.zeros((N1, W1 * CHIPS - 2 * GL), BF16)

    def hop(src, dst, send_sem, recv_sem, target, far):
        if far:
            return pltpu.make_async_remote_copy(
                src_ref=src, dst_ref=dst, send_sem=send_sem, recv_sem=recv_sem,
                device_id=(target, vert), device_id_type=MESH,
            )
        return pltpu.make_async_copy(src, dst, recv_sem)

    def first(unit, s, far):
        j = lax.rem(chip + s, CHIPS)
        if unit < GROUPS:
            src = send0.at[pl.ds(pl.multiple_of(16 * j, 16), 16), pl.ds(unit * GL, GL)]
            dst = mids[unit // 2].at[me]
            which = unit // 2
        else:
            src = send1.at[unit - GROUPS, :, pl.ds(pl.multiple_of(W1 * j, 128), W1)]
            dst = mids[2].at[me]
            which = 2
        return hop(src, dst, ps_sem.at[unit, s], pr_sem.at[which], 2 * j + unit % 2, far)

    def second(which, s, t, far):
        j = lax.rem(chip + s, CHIPS)
        k = 2 * j + t
        if which < 2:
            src = out0.at[which, k]
            g = 2 * which + core
            dst = recv0.at[pl.ds(pl.multiple_of(16 * chip, 16), 16), pl.ds(pl.multiple_of(g * GL, 128), GL)]
        else:
            src = out1.at[k]
            g = GROUPS + core
            dst = recv1.at[core, :, pl.ds(pl.multiple_of(W1 * chip, 128), W1)]
        return hop(src, dst, qs_sem.at[which, 2 * s + t], qr_sem.at[g], k, far)

    def start_first(unit):
        @pl.when(core == unit % 2)
        def _():
            first(unit, 0, False).start()

        @pl.when(core != unit % 2)
        def _():
            first(unit, 0, True).start()

        for s in range(1, CHIPS):
            first(unit, s, True).start()

    def start_second(which):
        mid, out = mids[which], out0.at[which] if which < 2 else out1
        pltpu.make_async_copy(mid, mid, pr_sem.at[which]).wait()

        @pl.loop(0, SECTORS)
        def _(k):
            out[k] = mid[kb_ref[k]]

        for s in range(1, CHIPS):
            for t in range(2):
                second(which, s, t, True).start()
        for t in range(2):
            @pl.when(core == t)
            def _():
                second(which, 0, t, False).start()

            @pl.when(core != t)
            def _():
                second(which, 0, t, True).start()

    for g in range(GROUPS):
        r_in(g).wait()
        parts = [jnp.dot(order, r_v[g * GROUP + i], preferred_element_type=F32).astype(BF16) for i in range(GROUP)]
        packed = jnp.concatenate(parts, axis=1)
        send0[:, g * GL:(g + 1) * GL] = packed[:N0]
        send1[g // 2, :, (g % 2) * GL:(g % 2 + 1) * GL] = packed[N0:]
        if g == 0:
            pl.semaphore_wait(barrier, SECTORS - 1 + 6)
        start_first(g)

    pair_row = jnp.concatenate(
        [jnp.full((1, V), occ_ref[pair_ref[0, p]] + occ_ref[pair_ref[1, p]], F32) for p in range(PAIRS)], axis=1
    )
    own_vir = own_vir_ref[pl.ds(me, 1), :]
    own_row = jnp.concatenate([own_vir] * PAIRS, axis=1)
    for r in range(R0 + R1):
        den[r:r + 1, :] = (pair_row - vir_ref[kb_ref[me], (R0 + R1) * vert + r]) - own_row

    t_in.wait()
    for q in range(PAIRS // QP):
        t_cat[q] = jnp.concatenate([t_v[q * QP + i] for i in range(QP)], axis=1)

    @pl.loop(0, GROUPS)
    def _(g):
        l_in(g).wait()

        @pl.loop(0, PAIRS // QP)
        def _(q):
            amps = t_cat[q]
            outs = []
            for i in range(GROUP):
                rows = pl.ds(pl.multiple_of(g * GL + i * V, 16), V)
                outs.append(jnp.dot(l_v[rows, :], amps, preferred_element_type=F32).astype(BF16))
            for i in range(QP):
                rows = pl.ds(pl.multiple_of(q * QP * V + i * V, 16), V)
                h[rows, pl.ds(pl.multiple_of(g * GL, 128), GL)] = jnp.concatenate(
                    [o[:, i * V:(i + 1) * V] for o in outs], axis=1
                )

        @pl.when(g == GROUPS // 2 - 1)
        def _():
            start_second(0)
            for half in range(2):
                start_first(GROUPS + half)

    start_second(1)

    def product(rows, right, half):
        return lax.dot_general(
            h[rows, half * 2 * GL:(half + 1) * 2 * GL], right, (((1,), (1,)), ((), ())), preferred_element_type=F32
        )

    def wait0(half):
        for g in (2 * half, 2 * half + 1):
            part = recv0.at[:, pl.ds(g * GL, GL)]
            pltpu.make_async_copy(part, part, qr_sem.at[g]).wait()

    def y_copy(part, s):
        src, dst = (ysend0, yrecv0) if part < 2 else (ysend1, yrecv1)
        return pltpu.make_async_remote_copy(
            src_ref=src.at[part % 2, lax.rem(y + s, 4)], dst_ref=dst.at[part % 2, s - 1],
            send_sem=ys_sem.at[part, s - 1], recv_sem=yr_sem.at[part, s - 1],
            device_id=y_peers[s - 1], device_id_type=MESH,
        )

    def z_copy(part, s):
        src, dst = (zsend0, zrecv0) if part < 2 else (zsend1, zrecv1)
        return pltpu.make_async_remote_copy(
            src_ref=src.at[part % 2, lax.rem(z + s, 4)], dst_ref=dst.at[part % 2, s - 1],
            send_sem=zs_sem.at[part, s - 1], recv_sem=zr_sem.at[part, s - 1],
            device_id=z_peers[s - 1], device_id_type=MESH,
        )

    def y_send(part):
        side = part % 2
        acc = acc0 if part < 2 else acc1

        @pl.loop(0, HALF // 128)
        def _(m):
            at = pl.ds(pl.multiple_of(m * 128, 128), 128)
            turned = acc[pl.ds(pl.multiple_of(side * HALF + m * 128, 128), 128), :].T
            if part < 2:
                full0[side, :, at] = turned
                for j in range(4):
                    ysend0[side, j, :, at] = turned[32 * j:32 * (j + 1)].astype(BF16)
            else:
                for j in range(4):
                    full1[side, j, 0:12, at] = turned[12 * j:12 * (j + 1)]

        if part >= 2:
            ysend1[side] = full1[side].astype(BF16)
        for s in (1, 2, 3):
            y_copy(part, s).start()

    def z_send(part):
        side = part % 2
        for s in (1, 2, 3):
            y_copy(part, s).wait()
        if part < 2:
            total = full0[side, pl.ds(pl.multiple_of(32 * y, 8), 32), :]
            for s in range(3):
                total = total + yrecv0[side, s].astype(F32)
            sum0[side] = total
            for j in range(4):
                zsend0[side, j] = jnp.concatenate(
                    [total[8 * j:8 * j + 8, :W2],
                     jnp.concatenate([total[8 * j:8 * j + 8, W2:], jnp.zeros((8, 2 * W2 - HALF), F32)], axis=1)], axis=0
                ).astype(BF16)
        else:
            total = full1[side, y]
            for s in range(3):
                total = total + yrecv1[side, s].astype(F32)
            for j in range(4):
                zsend1[side, j, 0:3, :] = total[3 * j:3 * j + 3, :W2]
                zsend1[side, j, 4:7, :HALF - W2] = total[3 * j:3 * j + 3, W2:]
        for s in (1, 2, 3):
            z_copy(part, s).start()

    def finish(part):
        side = part % 2
        at = side * HALF
        for s in (1, 2, 3):
            z_copy(part, s).wait()
        if part < 2:
            own = sum0[side, pl.ds(pl.multiple_of(8 * z, 8), 8), :]
            low, high = own[:, :W2], own[:, W2:]
            for s in range(3):
                got = zrecv0[side, s].astype(F32)
                low, high = low + got[0:8], high + got[8:16, :HALF - W2]
            rows = pl.ds(0, R0)
        else:
            last = zsend1[side, z]
            for s in range(3):
                last = last + zrecv1[side, s]
            low, high = last[0:R1], last[4:4 + R1, :HALF - W2]
            rows = pl.ds(R0, R1)
        o_ref[rows, at:at + W2] = low / den[rows, at:at + W2]
        o_ref[rows, at + W2:at + HALF] = high / den[rows, at + W2:at + HALF]

    full1[...] = jnp.zeros_like(full1)
    zsend1[...] = jnp.zeros_like(zsend1)

    wait0(0)

    @pl.loop(0, 4)
    def _(m):
        rows = pl.ds(pl.multiple_of(m * ROWS, 16), ROWS)
        acc0[rows, :] = product(rows, recv0[:, :2 * GL], 0)

    start_second(2)
    wait0(1)
    for side in range(2):
        @pl.loop(2 * side, 2 * side + 2)
        def _(m):
            rows = pl.ds(pl.multiple_of(m * ROWS, 16), ROWS)
            acc0[rows, :] += product(rows, recv0[:, 2 * GL:], 1)

        y_send(side)

    for half in range(2):
        pltpu.make_async_copy(recv1.at[half], recv1.at[half], qr_sem.at[GROUPS + half]).wait()
    for side in range(2):
        @pl.loop(2 * side, 2 * side + 2)
        def _(m):
            rows = pl.ds(pl.multiple_of(m * ROWS, 16), ROWS)
            acc1[rows, :] = product(rows, recv1[0, :, :2 * GL], 0) + product(rows, recv1[1, :, :2 * GL], 1)

        y_send(2 + side)
        z_send(side)

    z_send(2)
    z_send(3)
    for part in range(4):
        finish(part)

    for unit in range(GROUPS + 2):
        @pl.when(core != unit % 2)
        def _():
            first(unit, 0, True).wait_send()

        for s in range(1, CHIPS):
            first(unit, s, True).wait_send()
    for which in range(3):
        for t in range(2):
            @pl.when(core != t)
            def _():
                second(which, 0, t, True).wait_send()

            for s in range(1, CHIPS):
                second(which, s, t, True).wait_send()


def update_of(kb_table, pair_list, occ_energy, vir_energy, left, right, amps):
    any_space = pl.BlockSpec(memory_space=pl.ANY)
    smem = pl.BlockSpec(memory_space=pltpu.SMEM)
    vmem = pltpu.VMEM
    return pl.pallas_call(
        kernel,
        out_shape=jax.ShapeDtypeStruct((R0 + R1, PA), F32),
        in_specs=[smem] * 4 + [pl.BlockSpec(memory_space=pltpu.VMEM)] + [any_space] * 3,
        out_specs=pl.BlockSpec(memory_space=pltpu.VMEM),
        scratch_shapes=[
            vmem((KL, V), BF16), vmem((AUX, V, V), BF16), vmem((PAIRS, V, V), BF16),
            vmem((PAIRS // QP, V, QP * V), BF16),
            vmem((N0, KL), BF16), vmem((2, N1, W1 * CHIPS), BF16),
            vmem((SECTORS, 16, GL), BF16), vmem((SECTORS, 16, GL), BF16), vmem((SECTORS, N1, W1), BF16),
            vmem((2, SECTORS, 16, GL), BF16), vmem((SECTORS, N1, W1), BF16),
            vmem((N0, KL), BF16), vmem((2, N1, W1 * CHIPS), BF16), vmem((PA, KL), BF16),
            vmem((PA, N0), F32), vmem((PA, N1), F32), vmem((16, PA), F32),
            vmem((2, N0, HALF), F32), vmem((2, 4, 32, HALF), BF16), vmem((2, 3, 32, HALF), BF16),
            vmem((2, 32, HALF), F32), vmem((2, 4, 16, W2), BF16), vmem((2, 3, 16, W2), BF16),
            vmem((2, 4, 16, HALF), F32), vmem((2, 4, 16, HALF), BF16), vmem((2, 3, 16, HALF), BF16),
            vmem((2, 4, 8, W2), F32), vmem((2, 3, 8, W2), F32),
            pltpu.SemaphoreType.DMA((2 * GROUPS + 1,)),
            pltpu.SemaphoreType.DMA((GROUPS + 2, CHIPS)), pltpu.SemaphoreType.DMA((3,)),
            pltpu.SemaphoreType.DMA((3, SECTORS)), pltpu.SemaphoreType.DMA((GROUPS + 2,)),
            pltpu.SemaphoreType.DMA((4, 3)), pltpu.SemaphoreType.DMA((4, 3)),
            pltpu.SemaphoreType.DMA((4, 3)), pltpu.SemaphoreType.DMA((4, 3)),
        ],
        compiler_params=pltpu.CompilerParams(
            collective_id=0, has_side_effects=True, vmem_limit_bytes=60 * 2**20
        ),
    )(kb_table, pair_list, occ_energy, vir_energy, vir_energy, left, right, amps)


def on_device(left_factor, right_factor, amplitudes, kb_table, pair_list, occ_energy, vir_energy):
    left = left_factor.reshape(KL, V)
    right = right_factor.reshape(AUX, V, V)
    amps = amplitudes.reshape(PAIRS, V, V)
    update = update_of(kb_table, pair_list.T, occ_energy, vir_energy, left, right, amps)
    return update.reshape(1, R0 + R1, PAIRS, V)


def solution(mesh):
    placed = (
        P("ka", None, "vert", None, None),
        P("ka", None, "vert", None, None),
        P(),
        P(),
        P(),
        P(),
        P(),
    )
    return jax.shard_map(
        on_device,
        mesh=mesh,
        in_specs=placed,
        out_specs=P("ka", "vert", None, None),
        check_vma=False,
    )
```

```python
import jax
import jax.numpy as jnp
from jax import lax
from jax.experimental import pallas as pl
from jax.experimental.pallas import tpu as pltpu
from jax.sharding import PartitionSpec as P

MESH = pl.DeviceIdType.MESH
F32 = jnp.float32
BF16 = jnp.bfloat16

V = 176
AUX = 32
PAIRS = 16
SECTORS = 16
GROUP = 8
GROUPS = AUX // GROUP
GL = GROUP * V
KL = AUX * V
PA = PAIRS * V
WIDE = (768, 640, 768, 640)
FROM = (0, 768, 1408, 2176)
QP = 4
R0, R1 = 8, 3
N0, N1 = 16 * R0, 16 * R1
CHIPS = 8
W1 = 384


def kernel(kb_ref, pair_ref, occ_ref, vir_ref, own_vir_ref, l_hbm, r_hbm, t_hbm, o_ref,
           l_v, r_v, t_v, t_cat, send0, send1, mid_a, mid_b, mid_c, out0, out1, recv, h, acc, den,
           full, ysend, yrecv, zsum, zsend, zrecv,
           in_sem, ps_sem, pr_sem, qs_sem, qr_sem, ys_sem, yr_sem, zs_sem, zr_sem):
    me = lax.axis_index("ka")
    vert = lax.axis_index("vert")
    chip, core = me // 2, me % 2
    y, z = vert // 4, vert % 4
    y_peers = [(me, lax.rem(y + s, 4) * 4 + z) for s in (1, 2, 3)]
    z_peers = [(me, y * 4 + lax.rem(z + s, 4)) for s in (1, 2, 3)]

    barrier = pltpu.get_barrier_semaphore()
    for peer in y_peers + z_peers:
        pl.semaphore_signal(barrier, inc=1, device_id=peer, device_id_type=MESH)

    @pl.loop(1, SECTORS)
    def _(s):
        pl.semaphore_signal(barrier, inc=1, device_id=(lax.rem(me + s, SECTORS), vert), device_id_type=MESH)

    def r_in(g):
        return pltpu.make_async_copy(r_hbm.at[pl.ds(g * GROUP, GROUP)], r_v.at[pl.ds(g * GROUP, GROUP)], in_sem.at[g])

    def l_in(g):
        rows = pl.ds(pl.multiple_of(g * GL, 16), GL)
        return pltpu.make_async_copy(l_hbm.at[rows], l_v.at[rows], in_sem.at[GROUPS + g])

    t_in = pltpu.make_async_copy(t_hbm, t_v, in_sem.at[2 * GROUPS])
    for g in range(GROUPS):
        r_in(g).start()
    t_in.start()
    for g in range(GROUPS):
        l_in(g).start()

    mids = (mid_a, mid_b, mid_c)

    row = lax.broadcasted_iota(jnp.int32, (V, V), 0)
    col = lax.broadcasted_iota(jnp.int32, (V, V), 1)
    late = row - N0
    third = lax.shift_right_logical(late * 21846, 16)
    source = jnp.where(row < N0, 11 * lax.shift_right_logical(row, 3) + (row & 7), 11 * third + R0 + (late - 3 * third))
    order = (col == source).astype(F32).astype(BF16)

    for half in range(2):
        send1[half, :, 2 * GL:] = jnp.zeros((N1, W1 * CHIPS - 2 * GL), BF16)

    def hop(src, dst, send_sem, recv_sem, target, far):
        if far:
            return pltpu.make_async_remote_copy(
                src_ref=src, dst_ref=dst, send_sem=send_sem, recv_sem=recv_sem,
                device_id=(target, vert), device_id_type=MESH,
            )
        return pltpu.make_async_copy(src, dst, recv_sem)

    def first(unit, s, far):
        j = lax.rem(chip + s, CHIPS)
        if unit < GROUPS:
            src = send0.at[pl.ds(pl.multiple_of(16 * j, 16), 16), pl.ds(unit * GL, GL)]
            dst = mids[unit // 2].at[me]
            which = unit // 2
        else:
            src = send1.at[unit - GROUPS, :, pl.ds(pl.multiple_of(W1 * j, 128), W1)]
            dst = mids[2].at[me]
            which = 2
        return hop(src, dst, ps_sem.at[unit, s], pr_sem.at[which], 2 * j + unit % 2, far)

    def second(which, s, t, far):
        j = lax.rem(chip + s, CHIPS)
        k = 2 * j + t
        if which < 2:
            src = out0.at[which, k]
            g = 2 * which + core
            dst = recv.at[which, pl.ds(pl.multiple_of(16 * chip, 16), 16), pl.ds(pl.multiple_of(core * GL, 128), GL)]
        else:
            src = out1.at[k]
            g = GROUPS + core
            dst = recv.at[core, pl.ds(N0, N1), pl.ds(pl.multiple_of(W1 * chip, 128), W1)]
        return hop(src, dst, qs_sem.at[which, 2 * s + t], qr_sem.at[g], k, far)

    def start_first(unit):
        @pl.when(core == unit % 2)
        def _():
            first(unit, 0, False).start()

        @pl.when(core != unit % 2)
        def _():
            first(unit, 0, True).start()

        for s in range(1, CHIPS):
            first(unit, s, True).start()

    def start_second(which):
        mid, out = mids[which], out0.at[which] if which < 2 else out1
        pltpu.make_async_copy(mid, mid, pr_sem.at[which]).wait()

        @pl.loop(0, SECTORS)
        def _(k):
            out[k] = mid[kb_ref[k]]

        for s in range(1, CHIPS):
            for t in range(2):
                second(which, s, t, True).start()
        for t in range(2):
            @pl.when(core == t)
            def _():
                second(which, 0, t, False).start()

            @pl.when(core != t)
            def _():
                second(which, 0, t, True).start()

    for g in range(GROUPS):
        r_in(g).wait()
        parts = [jnp.dot(order, r_v[g * GROUP + i], preferred_element_type=F32).astype(BF16) for i in range(GROUP)]
        packed = jnp.concatenate(parts, axis=1)
        send0[:, g * GL:(g + 1) * GL] = packed[:N0]
        send1[g // 2, :, (g % 2) * GL:(g % 2 + 1) * GL] = packed[N0:]
        if g == 0:
            pl.semaphore_wait(barrier, SECTORS - 1 + 6)
        if g < 2:
            start_first(g)
    for unit in (GROUPS, GROUPS + 1, 2, 3):
        start_first(unit)

    pair_row = jnp.concatenate(
        [jnp.full((1, V), occ_ref[pair_ref[0, p]] + occ_ref[pair_ref[1, p]], F32) for p in range(PAIRS)], axis=1
    )
    own_vir = own_vir_ref[pl.ds(me, 1), :]
    own_row = jnp.concatenate([own_vir] * PAIRS, axis=1)
    for r in range(R0 + R1):
        den[r:r + 1, :] = (pair_row - vir_ref[kb_ref[me], (R0 + R1) * vert + r]) - own_row

    t_in.wait()
    for q in range(PAIRS // QP):
        t_cat[q] = jnp.concatenate([t_v[q * QP + i] for i in range(QP)], axis=1)

    @pl.loop(0, GROUPS)
    def _(g):
        l_in(g).wait()

        @pl.loop(0, PAIRS // QP)
        def _(q):
            amps = t_cat[q]
            outs = []
            for i in range(GROUP):
                rows = pl.ds(pl.multiple_of(g * GL + i * V, 16), V)
                outs.append(jnp.dot(l_v[rows, :], amps, preferred_element_type=F32).astype(BF16))
            for i in range(QP):
                rows = pl.ds(pl.multiple_of(q * QP * V + i * V, 16), V)
                h[rows, pl.ds(pl.multiple_of(g * GL, 128), GL)] = jnp.concatenate(
                    [o[:, i * V:(i + 1) * V] for o in outs], axis=1
                )

        @pl.when(g == GROUPS // 2 - 1)
        def _():
            start_second(0)

        @pl.when(g == GROUPS // 2)
        def _():
            start_second(2)

    start_second(1)

    def arrive(half):
        for g in range(2):
            part = recv.at[half, pl.ds(0, N0), pl.ds(g * GL, GL)]
            pltpu.make_async_copy(part, part, qr_sem.at[2 * half + g]).wait()
        part = recv.at[half, pl.ds(N0, N1), :]
        pltpu.make_async_copy(part, part, qr_sem.at[GROUPS + half]).wait()

    def product(rows, half):
        return lax.dot_general(
            h[rows, half * 2 * GL:(half + 1) * 2 * GL], recv[half, :, :2 * GL], (((1,), (1,)), ((), ())),
            preferred_element_type=F32,
        )

    def y_copy(part, s):
        return pltpu.make_async_remote_copy(
            src_ref=ysend.at[part, lax.rem(y + s, 4), :, pl.ds(0, WIDE[part])],
            dst_ref=yrecv.at[part, s - 1, :, pl.ds(0, WIDE[part])],
            send_sem=ys_sem.at[part, s - 1], recv_sem=yr_sem.at[part, s - 1],
            device_id=y_peers[s - 1], device_id_type=MESH,
        )

    def z_copy(part, s):
        return pltpu.make_async_remote_copy(
            src_ref=zsend.at[part, lax.rem(z + s, 4), :, pl.ds(0, WIDE[part])],
            dst_ref=zrecv.at[part, s - 1, :, pl.ds(0, WIDE[part])],
            send_sem=zs_sem.at[part, s - 1], recv_sem=zr_sem.at[part, s - 1],
            device_id=z_peers[s - 1], device_id_type=MESH,
        )

    def y_send(part):
        for m in range(WIDE[part] // 128):
            at = slice(m * 128, (m + 1) * 128)
            rows = slice(FROM[part] + m * 128, FROM[part] + (m + 1) * 128)
            early, late = acc[rows, :N0].T, acc[rows, N0:].T
            for j in range(4):
                full[part, j, 0:32, at] = early[32 * j:32 * (j + 1)]
                full[part, j, 32:44, at] = late[12 * j:12 * (j + 1)]
        for j in range(4):
            ysend[part, j] = full[part, j].astype(BF16)
        for s in (1, 2, 3):
            y_copy(part, s).start()

    def z_send(part):
        w = WIDE[part]
        for s in (1, 2, 3):
            y_copy(part, s).wait()
        total = full[part, y, :, :w]
        for s in range(3):
            total = total + yrecv[part, s, :, :w].astype(F32)
        for j in range(4):
            zsum[part, j, 0:8, :w] = total[8 * j:8 * j + 8]
            zsum[part, j, 8:11, :w] = total[32 + 3 * j:35 + 3 * j]
        for j in range(4):
            zsend[part, j] = zsum[part, j].astype(BF16)
        for s in (1, 2, 3):
            z_copy(part, s).start()

    def finish(part):
        w, at = WIDE[part], FROM[part]
        for s in (1, 2, 3):
            z_copy(part, s).wait()
        total = zsum[part, z, :, :w]
        for s in range(3):
            total = total + zrecv[part, s, :, :w].astype(F32)
        o_ref[:, at:at + w] = total[:R0 + R1] / den[:R0 + R1, at:at + w]

    full[...] = jnp.zeros_like(full)
    zsum[...] = jnp.zeros_like(zsum)

    arrive(0)

    @pl.loop(0, 4)
    def _(m):
        rows = pl.ds(pl.multiple_of(m * (PA // 4), 16), PA // 4)
        acc[rows, :] = product(rows, 0)

    arrive(1)
    for part in range(4):
        rows = slice(FROM[part], FROM[part] + WIDE[part])
        acc[rows, :] += product(rows, 1)
        y_send(part)
    for part in range(4):
        z_send(part)
        if part > 0:
            finish(part - 1)
    finish(3)

    for unit in range(GROUPS + 2):
        @pl.when(core != unit % 2)
        def _():
            first(unit, 0, True).wait_send()

        for s in range(1, CHIPS):
            first(unit, s, True).wait_send()
    for which in range(3):
        for t in range(2):
            @pl.when(core != t)
            def _():
                second(which, 0, t, True).wait_send()

            for s in range(1, CHIPS):
                second(which, s, t, True).wait_send()


def update_of(kb_table, pair_list, occ_energy, vir_energy, left, right, amps):
    any_space = pl.BlockSpec(memory_space=pl.ANY)
    smem = pl.BlockSpec(memory_space=pltpu.SMEM)
    vmem = pltpu.VMEM
    return pl.pallas_call(
        kernel,
        out_shape=jax.ShapeDtypeStruct((R0 + R1, PA), F32),
        in_specs=[smem] * 4 + [pl.BlockSpec(memory_space=pltpu.VMEM)] + [any_space] * 3,
        out_specs=pl.BlockSpec(memory_space=pltpu.VMEM),
        scratch_shapes=[
            vmem((KL, V), BF16), vmem((AUX, V, V), BF16), vmem((PAIRS, V, V), BF16),
            vmem((PAIRS // QP, V, QP * V), BF16),
            vmem((N0, KL), BF16), vmem((2, N1, W1 * CHIPS), BF16),
            vmem((SECTORS, 16, GL), BF16), vmem((SECTORS, 16, GL), BF16), vmem((SECTORS, N1, W1), BF16),
            vmem((2, SECTORS, 16, GL), BF16), vmem((SECTORS, N1, W1), BF16),
            vmem((2, V, W1 * CHIPS), BF16), vmem((PA, KL), BF16), vmem((PA, V), F32), vmem((16, PA), F32),
            vmem((4, 4, 48, 768), F32), vmem((4, 4, 48, 768), BF16), vmem((4, 3, 48, 768), BF16),
            vmem((4, 4, 16, 768), F32), vmem((4, 4, 16, 768), BF16), vmem((4, 3, 16, 768), BF16),
            pltpu.SemaphoreType.DMA((2 * GROUPS + 1,)),
            pltpu.SemaphoreType.DMA((GROUPS + 2, CHIPS)), pltpu.SemaphoreType.DMA((3,)),
            pltpu.SemaphoreType.DMA((3, SECTORS)), pltpu.SemaphoreType.DMA((GROUPS + 2,)),
            pltpu.SemaphoreType.DMA((4, 3)), pltpu.SemaphoreType.DMA((4, 3)),
            pltpu.SemaphoreType.DMA((4, 3)), pltpu.SemaphoreType.DMA((4, 3)),
        ],
        compiler_params=pltpu.CompilerParams(
            collective_id=0, has_side_effects=True, vmem_limit_bytes=60 * 2**20
        ),
    )(kb_table, pair_list, occ_energy, vir_energy, vir_energy, left, right, amps)


def on_device(left_factor, right_factor, amplitudes, kb_table, pair_list, occ_energy, vir_energy):
    left = left_factor.reshape(KL, V)
    right = right_factor.reshape(AUX, V, V)
    amps = amplitudes.reshape(PAIRS, V, V)
    update = update_of(kb_table, pair_list.T, occ_energy, vir_energy, left, right, amps)
    return update.reshape(1, R0 + R1, PAIRS, V)


def solution(mesh):
    placed = (
        P("ka", None, "vert", None, None),
        P("ka", None, "vert", None, None),
        P(),
        P(),
        P(),
        P(),
        P(),
    )
    return jax.shard_map(
        on_device,
        mesh=mesh,
        in_specs=placed,
        out_specs=P("ka", "vert", None, None),
        check_vma=False,
    )
```

```python
import jax
import jax.numpy as jnp
from jax import lax
from jax.experimental import pallas as pl
from jax.experimental.pallas import tpu as pltpu
from jax.sharding import PartitionSpec as P

MESH = pl.DeviceIdType.MESH
F32 = jnp.float32
BF16 = jnp.bfloat16

V = 176
AUX = 32
PAIRS = 16
SECTORS = 16
GROUP = 8
GROUPS = AUX // GROUP
GL = GROUP * V
KL = AUX * V
PA = PAIRS * V
WIDE = (896, 896, 640, 384)
FROM = (0, 896, 1792, 2432)
ZWIDE = (896, 640, 896)
QP = 4
R0, R1 = 8, 3
N0, N1 = 16 * R0, 16 * R1
CHIPS = 8
W1 = 384


def kernel(kb_ref, pair_ref, occ_ref, vir_ref, own_vir_ref, l_hbm, r_hbm, t_hbm, o_ref,
           l_v, r_v, t_v, t_cat, send0, send1, mid_a, mid_b, mid_c, out0, out1, recv, h, acc_f, acc_l, den,
           full, ysend, yrecv, zsum, zsend, zrecv,
           in_sem, ps_sem, pr_sem, qs_sem, qr_sem, ys_sem, yr_sem, zs_sem, zr_sem):
    me = lax.axis_index("ka")
    vert = lax.axis_index("vert")
    chip, core = me // 2, me % 2
    y, z = vert // 4, vert % 4
    y_peers = [(me, lax.rem(y + s, 4) * 4 + z) for s in (1, 2, 3)]
    z_peers = [(me, y * 4 + lax.rem(z + s, 4)) for s in (1, 2, 3)]

    def r_in(g):
        return pltpu.make_async_copy(r_hbm.at[pl.ds(g * GROUP, GROUP)], r_v.at[pl.ds(g * GROUP, GROUP)], in_sem.at[g])

    def l_in(g):
        rows = pl.ds(pl.multiple_of(g * GL, 16), GL)
        return pltpu.make_async_copy(l_hbm.at[rows], l_v.at[rows], in_sem.at[GROUPS + g])

    t_in = pltpu.make_async_copy(t_hbm, t_v, in_sem.at[2 * GROUPS])
    for g in range(GROUPS):
        r_in(g).start()
    t_in.start()
    for g in range(GROUPS):
        l_in(g).start()

    barrier = pltpu.get_barrier_semaphore()
    for peer in y_peers + z_peers:
        pl.semaphore_signal(barrier, inc=1, device_id=peer, device_id_type=MESH)

    @pl.loop(1, SECTORS)
    def _(s):
        pl.semaphore_signal(barrier, inc=1, device_id=(lax.rem(me + s, SECTORS), vert), device_id_type=MESH)

    mids = (mid_a, mid_b, mid_c)

    row = lax.broadcasted_iota(jnp.int32, (V, V), 0)
    col = lax.broadcasted_iota(jnp.int32, (V, V), 1)
    late = row - N0
    third = lax.shift_right_logical(late * 21846, 16)
    source = jnp.where(
        row < N0,
        11 * lax.shift_right_logical(row & 63, 2) + (row & 3) + 4 * lax.shift_right_logical(row, 6),
        11 * third + R0 + (late - 3 * third),
    )
    order = (col == source).astype(F32).astype(BF16)

    for half in range(2):
        send1[half, :, 2 * GL:] = jnp.zeros((N1, W1 * CHIPS - 2 * GL), BF16)

    def hop(src, dst, send_sem, recv_sem, target, far):
        if far:
            return pltpu.make_async_remote_copy(
                src_ref=src, dst_ref=dst, send_sem=send_sem, recv_sem=recv_sem,
                device_id=(target, vert), device_id_type=MESH,
            )
        return pltpu.make_async_copy(src, dst, recv_sem)

    def first(unit, s, far):
        j = lax.rem(chip + s, CHIPS)
        if unit < GROUPS:
            g = 2 * (unit % 2) + j // 4
            src = send0.at[pl.ds(pl.multiple_of(64 * (unit // 2) + 16 * lax.rem(j, 4), 16), 16), pl.ds(pl.multiple_of(g * GL, 128), GL)]
            dst = mids[unit // 2].at[me]
            which = unit // 2
        else:
            src = send1.at[unit - GROUPS, :, pl.ds(pl.multiple_of(W1 * j, 128), W1)]
            dst = mids[2].at[me]
            which = 2
        return hop(src, dst, ps_sem.at[unit, s], pr_sem.at[which], 2 * j + unit % 2, far)

    def second(which, s, t, far):
        j = lax.rem(chip + s, CHIPS)
        k = 2 * j + t
        if which < 2:
            src = out0.at[which, k]
            g = 2 * which + core
            rows = pl.ds(pl.multiple_of(64 * which + 16 * lax.rem(chip, 4), 16), 16)
            dst = recv.at[core, rows, pl.ds(pl.multiple_of(chip // 4 * GL, 128), GL)]
        else:
            src = out1.at[k]
            g = GROUPS + core
            dst = recv.at[core, pl.ds(N0, N1), pl.ds(pl.multiple_of(W1 * chip, 128), W1)]
        return hop(src, dst, qs_sem.at[which, 2 * s + t], qr_sem.at[g], k, far)

    def start_first(unit):
        @pl.when(core == unit % 2)
        def _():
            first(unit, 0, False).start()

        @pl.when(core != unit % 2)
        def _():
            first(unit, 0, True).start()

        for s in range(1, CHIPS):
            first(unit, s, True).start()

    def start_second(which):
        mid, out = mids[which], out0.at[which] if which < 2 else out1
        pltpu.make_async_copy(mid, mid, pr_sem.at[which]).wait()

        @pl.loop(0, SECTORS)
        def _(k):
            out[k] = mid[kb_ref[k]]

        for s in range(1, CHIPS):
            for t in range(2):
                second(which, s, t, True).start()
        for t in range(2):
            @pl.when(core == t)
            def _():
                second(which, 0, t, False).start()

            @pl.when(core != t)
            def _():
                second(which, 0, t, True).start()

    for g in range(GROUPS):
        r_in(g).wait()
        parts = [jnp.dot(order, r_v[g * GROUP + i], preferred_element_type=F32).astype(BF16) for i in range(GROUP)]
        packed = jnp.concatenate(parts, axis=1)
        send0[:, g * GL:(g + 1) * GL] = packed[:N0]
        send1[g // 2, :, (g % 2) * GL:(g % 2 + 1) * GL] = packed[N0:]
        if g == 0:
            pl.semaphore_wait(barrier, SECTORS - 1 + 6)
        if g % 2 == 1:
            start_first(g // 2)
    for unit in (GROUPS, GROUPS + 1, 2, 3):
        start_first(unit)

    pair_row = jnp.concatenate(
        [jnp.full((1, V), occ_ref[pair_ref[0, p]] + occ_ref[pair_ref[1, p]], F32) for p in range(PAIRS)], axis=1
    )
    own_vir = own_vir_ref[pl.ds(me, 1), :]
    own_row = jnp.concatenate([own_vir] * PAIRS, axis=1)
    for r in range(R0 + R1):
        den[r:r + 1, :] = (pair_row - vir_ref[kb_ref[me], (R0 + R1) * vert + r]) - own_row

    t_in.wait()
    for q in range(PAIRS // QP):
        t_cat[q] = jnp.concatenate([t_v[q * QP + i] for i in range(QP)], axis=1)

    @pl.loop(0, GROUPS)
    def _(g):
        l_in(g).wait()

        @pl.loop(0, PAIRS // QP)
        def _(q):
            amps = t_cat[q]
            outs = []
            for i in range(GROUP):
                rows = pl.ds(pl.multiple_of(g * GL + i * V, 16), V)
                outs.append(jnp.dot(l_v[rows, :], amps, preferred_element_type=F32).astype(BF16))
            for i in range(QP):
                rows = pl.ds(pl.multiple_of(q * QP * V + i * V, 16), V)
                h[rows, pl.ds(pl.multiple_of(g * GL, 128), GL)] = jnp.concatenate(
                    [o[:, i * V:(i + 1) * V] for o in outs], axis=1
                )

        @pl.when(g == GROUPS // 2 - 1)
        def _():
            start_second(0)

        @pl.when(g == GROUPS // 2)
        def _():
            start_second(2)

    start_second(1)

    def sent_first():
        for unit in range(GROUPS + 2):
            @pl.when(core != unit % 2)
            def _():
                first(unit, 0, True).wait_send()

            for s in range(1, CHIPS):
                first(unit, s, True).wait_send()

    def sent_second(which):
        for t in range(2):
            @pl.when(core != t)
            def _():
                second(which, 0, t, True).wait_send()

            for s in range(1, CHIPS):
                second(which, s, t, True).wait_send()

    def arrive(unit, rows, lanes):
        for half in range(2):
            part = recv.at[half, rows, lanes]
            pltpu.make_async_copy(part, part, qr_sem.at[unit + half]).wait()

    def product(rows, b_from, b_to):
        terms = [
            lax.dot_general(
                h[rows, half * 2 * GL:(half + 1) * 2 * GL], recv[half, b_from:b_to, :2 * GL], (((1,), (1,)), ((), ())),
                preferred_element_type=F32,
            )
            for half in range(2)
        ]
        return terms[0] + terms[1]

    def y_copy(part, s, last):
        rows = pl.ds(16, 32) if last else pl.ds(0, 16)
        return pltpu.make_async_remote_copy(
            src_ref=ysend.at[part, lax.rem(y + s, 4), rows, pl.ds(0, WIDE[part])],
            dst_ref=yrecv.at[part, s - 1, rows, pl.ds(0, WIDE[part])],
            send_sem=ys_sem.at[last, part, s - 1], recv_sem=yr_sem.at[last, part, s - 1],
            device_id=y_peers[s - 1], device_id_type=MESH,
        )

    def z_copy(pack, s):
        return pltpu.make_async_remote_copy(
            src_ref=zsend.at[pack, lax.rem(z + s, 4), :, pl.ds(0, ZWIDE[pack])],
            dst_ref=zrecv.at[pack, s - 1, :, pl.ds(0, ZWIDE[pack])],
            send_sem=zs_sem.at[pack, s - 1], recv_sem=zr_sem.at[pack, s - 1],
            device_id=z_peers[s - 1], device_id_type=MESH,
        )

    def y_send(part, last):
        @pl.loop(0, WIDE[part] // 128)
        def _(m):
            at = pl.ds(pl.multiple_of(m * 128, 128), 128)
            rows = pl.ds(pl.multiple_of(FROM[part] + m * 128, 128), 128)
            if last:
                turned = acc_l[rows, :].T
                for j in range(4):
                    full[part, j, 16:32, at] = turned[16 * j:16 * (j + 1)]
                    full[part, j, 32:44, at] = turned[64 + 12 * j:64 + 12 * (j + 1)]
            else:
                turned = acc_f[rows, :].T
                for j in range(4):
                    full[part, j, 0:16, at] = turned[16 * j:16 * (j + 1)]

        own = slice(16, 48) if last else slice(0, 16)
        for j in range(4):
            ysend[part, j, own] = full[part, j, own].astype(BF16)
        for s in (1, 2, 3):
            y_copy(part, s, last).start()

    def y_sum(part, last):
        w = WIDE[part]
        rows = slice(16, 48) if last else slice(0, 16)
        for s in (1, 2, 3):
            y_copy(part, s, last).wait()
        total = full[part, y, rows, :w]
        for s in range(3):
            total = total + yrecv[part, s, rows, :w].astype(F32)
        for j in range(4):
            if last:
                at = 8 * (part % 2)
                zsum[part // 2, j, at:at + 4, :w] = total[4 * j:4 * j + 4]
                zsum[part // 2, j, at + 4:at + 7, :w] = total[16 + 3 * j:19 + 3 * j]
            else:
                zsum[2, j, 4 * part:4 * part + 4, :w] = total[4 * j:4 * j + 4]

    def z_send(pack):
        for j in range(4):
            zsend[pack, j] = zsum[pack, j].astype(BF16)
        for s in (1, 2, 3):
            z_copy(pack, s).start()

    def finish(pack):
        for s in (1, 2, 3):
            z_copy(pack, s).wait()
        total = zsum[pack, z, :, :ZWIDE[pack]]
        for s in range(3):
            total = total + zrecv[pack, s, :, :ZWIDE[pack]].astype(F32)
        for part in ((2 * pack, 2 * pack + 1) if pack < 2 else range(4)):
            w, at = WIDE[part], FROM[part]
            if pack < 2:
                o_ref[4:11, at:at + w] = total[8 * (part % 2):8 * (part % 2) + 7, :w] / den[4:11, at:at + w]
            else:
                o_ref[0:4, at:at + w] = total[4 * part:4 * part + 4, :w] / den[0:4, at:at + w]

    full[...] = jnp.zeros_like(full)
    zsum[...] = jnp.zeros_like(zsum)

    sent_first()
    arrive(0, pl.ds(0, 64), pl.ds(0, 2 * GL))

    @pl.loop(0, 4)
    def _(m):
        rows = pl.ds(pl.multiple_of(m * (PA // 4), 16), PA // 4)
        acc_f[rows, :] = product(rows, 0, 64)

    for part in range(4):
        y_send(part, 0)
    sent_second(0)
    arrive(GROUPS, pl.ds(N0, N1), slice(None))
    sent_second(2)
    arrive(2, pl.ds(64, 64), pl.ds(0, 2 * GL))
    for part in range(4):
        @pl.loop(0, 2)
        def _(m):
            rows = pl.ds(pl.multiple_of(FROM[part] + m * (WIDE[part] // 2), 64), WIDE[part] // 2)
            acc_l[rows, :] = product(rows, 64, V)

        y_send(part, 1)
        if part == 1:
            for first_part in range(4):
                y_sum(first_part, 0)
            z_send(2)
        if part == 2:
            for early_part in range(2):
                y_sum(early_part, 1)
            z_send(0)
    sent_second(1)
    finish(2)
    y_sum(2, 1)
    y_sum(3, 1)
    z_send(1)
    finish(0)
    finish(1)


def update_of(kb_table, pair_list, occ_energy, vir_energy, left, right, amps):
    any_space = pl.BlockSpec(memory_space=pl.ANY)
    smem = pl.BlockSpec(memory_space=pltpu.SMEM)
    vmem = pltpu.VMEM
    return pl.pallas_call(
        kernel,
        out_shape=jax.ShapeDtypeStruct((R0 + R1, PA), F32),
        in_specs=[smem] * 4 + [pl.BlockSpec(memory_space=pltpu.VMEM)] + [any_space] * 3,
        out_specs=pl.BlockSpec(memory_space=pltpu.VMEM),
        scratch_shapes=[
            vmem((KL, V), BF16), vmem((AUX, V, V), BF16), vmem((PAIRS, V, V), BF16),
            vmem((PAIRS // QP, V, QP * V), BF16),
            vmem((N0, KL), BF16), vmem((2, N1, W1 * CHIPS), BF16),
            vmem((SECTORS, 16, GL), BF16), vmem((SECTORS, 16, GL), BF16), vmem((SECTORS, N1, W1), BF16),
            vmem((2, SECTORS, 16, GL), BF16), vmem((SECTORS, N1, W1), BF16),
            vmem((2, V, W1 * CHIPS), BF16), vmem((PA, KL), BF16), vmem((PA, 64), F32), vmem((PA, V - 64), F32),
            vmem((16, PA), F32),
            vmem((4, 4, 48, 896), F32), vmem((4, 4, 48, 896), BF16), vmem((4, 3, 48, 896), BF16),
            vmem((3, 4, 16, 896), F32), vmem((3, 4, 16, 896), BF16), vmem((3, 3, 16, 896), BF16),
            pltpu.SemaphoreType.DMA((2 * GROUPS + 1,)),
            pltpu.SemaphoreType.DMA((GROUPS + 2, CHIPS)), pltpu.SemaphoreType.DMA((3,)),
            pltpu.SemaphoreType.DMA((3, SECTORS)), pltpu.SemaphoreType.DMA((GROUPS + 2,)),
            pltpu.SemaphoreType.DMA((2, 4, 3)), pltpu.SemaphoreType.DMA((2, 4, 3)),
            pltpu.SemaphoreType.DMA((3, 3)), pltpu.SemaphoreType.DMA((3, 3)),
        ],
        compiler_params=pltpu.CompilerParams(
            collective_id=0, has_side_effects=True, vmem_limit_bytes=60 * 2**20
        ),
    )(kb_table, pair_list, occ_energy, vir_energy, vir_energy, left, right, amps)


def on_device(left_factor, right_factor, amplitudes, kb_table, pair_list, occ_energy, vir_energy):
    left = left_factor.reshape(KL, V)
    right = right_factor.reshape(AUX, V, V)
    amps = amplitudes.reshape(PAIRS, V, V)
    update = update_of(kb_table, pair_list.T, occ_energy, vir_energy, left, right, amps)
    return update.reshape(1, R0 + R1, PAIRS, V)


def solution(mesh):
    placed = (
        P("ka", None, "vert", None, None),
        P("ka", None, "vert", None, None),
        P(),
        P(),
        P(),
        P(),
        P(),
    )
    return jax.shard_map(
        on_device,
        mesh=mesh,
        in_specs=placed,
        out_specs=P("ka", "vert", None, None),
        check_vma=False,
    )
```

```python
import jax
import jax.numpy as jnp
from jax import lax
from jax.experimental import pallas as pl
from jax.experimental.pallas import tpu as pltpu
from jax.sharding import PartitionSpec as P

MESH = pl.DeviceIdType.MESH
F32 = jnp.float32
BF16 = jnp.bfloat16

V = 176
AUX = 32
PAIRS = 16
SECTORS = 16
GROUP = 8
GROUPS = AUX // GROUP
GL = GROUP * V
KL = AUX * V
PA = PAIRS * V
WIDE = (512, 896, 896, 512)
FROM = (0, 512, 1408, 2304)
QP = 4
R0, R1 = 8, 3
N0, N1 = 16 * R0, 16 * R1
CHIPS = 8
W1 = 384


def kernel(kb_ref, pair_ref, occ_ref, vir_ref, own_vir_ref, l_hbm, r_hbm, t_hbm, o_ref,
           l_v, r_v, t_v, t_cat, send0, send1, mid_a, mid_b, mid_c, out0, out1, recv, h, acc, den,
           full, ysend, yrecv, zsum, zsend, zrecv,
           in_sem, ps_sem, pr_sem, qs_sem, qr_sem, ys_sem, yr_sem, zs_sem, zr_sem):
    me = lax.axis_index("ka")
    vert = lax.axis_index("vert")
    chip, core = me // 2, me % 2
    y, z = vert // 4, vert % 4
    y_peers = [(me, lax.rem(y + s, 4) * 4 + z) for s in (1, 2, 3)]
    z_peers = [(me, y * 4 + lax.rem(z + s, 4)) for s in (1, 2, 3)]

    def r_in(g):
        return pltpu.make_async_copy(r_hbm.at[pl.ds(g * GROUP, GROUP)], r_v.at[pl.ds(g * GROUP, GROUP)], in_sem.at[g])

    def l_in(g):
        rows = pl.ds(pl.multiple_of(g * GL, 16), GL)
        return pltpu.make_async_copy(l_hbm.at[rows], l_v.at[rows], in_sem.at[GROUPS + g])

    t_in = pltpu.make_async_copy(t_hbm, t_v, in_sem.at[2 * GROUPS])
    for g in range(GROUPS):
        r_in(g).start()
    t_in.start()
    for g in range(GROUPS):
        l_in(g).start()

    barrier = pltpu.get_barrier_semaphore()
    for peer in y_peers + z_peers:
        pl.semaphore_signal(barrier, inc=1, device_id=peer, device_id_type=MESH)

    @pl.loop(1, SECTORS)
    def _(s):
        pl.semaphore_signal(barrier, inc=1, device_id=(lax.rem(me + s, SECTORS), vert), device_id_type=MESH)

    mids = (mid_a, mid_b, mid_c)

    row = lax.broadcasted_iota(jnp.int32, (V, V), 0)
    col = lax.broadcasted_iota(jnp.int32, (V, V), 1)
    late = row - N0
    third = lax.shift_right_logical(late * 21846, 16)
    source = jnp.where(row < N0, 11 * lax.shift_right_logical(row, 3) + (row & 7), 11 * third + R0 + (late - 3 * third))
    order = (col == source).astype(F32).astype(BF16)

    for half in range(2):
        send1[half, :, 2 * GL:] = jnp.zeros((N1, W1 * CHIPS - 2 * GL), BF16)

    def hop(src, dst, send_sem, recv_sem, target, far):
        if far:
            return pltpu.make_async_remote_copy(
                src_ref=src, dst_ref=dst, send_sem=send_sem, recv_sem=recv_sem,
                device_id=(target, vert), device_id_type=MESH,
            )
        return pltpu.make_async_copy(src, dst, recv_sem)

    def first(unit, s, far):
        j = lax.rem(chip + s, CHIPS)
        if unit < GROUPS:
            src = send0.at[pl.ds(pl.multiple_of(16 * j, 16), 16), pl.ds(unit * GL, GL)]
            dst = mids[unit // 2].at[me]
            which = unit // 2
        else:
            src = send1.at[unit - GROUPS, :, pl.ds(pl.multiple_of(W1 * j, 128), W1)]
            dst = mids[2].at[me]
            which = 2
        return hop(src, dst, ps_sem.at[unit, s], pr_sem.at[which], 2 * j + unit % 2, far)

    def second(which, s, t, far):
        j = lax.rem(chip + s, CHIPS)
        k = 2 * j + t
        if which < 2:
            src = out0.at[which, k]
            g = 2 * which + core
            dst = recv.at[which, pl.ds(pl.multiple_of(16 * chip, 16), 16), pl.ds(pl.multiple_of(core * GL, 128), GL)]
        else:
            src = out1.at[k]
            g = GROUPS + core
            dst = recv.at[core, pl.ds(N0, N1), pl.ds(pl.multiple_of(W1 * chip, 128), W1)]
        return hop(src, dst, qs_sem.at[which, 2 * s + t], qr_sem.at[g], k, far)

    def start_first(unit):
        @pl.when(core == unit % 2)
        def _():
            first(unit, 0, False).start()

        @pl.when(core != unit % 2)
        def _():
            first(unit, 0, True).start()

        for s in range(1, CHIPS):
            first(unit, s, True).start()

    def start_second(which):
        mid, out = mids[which], out0.at[which] if which < 2 else out1
        pltpu.make_async_copy(mid, mid, pr_sem.at[which]).wait()

        @pl.loop(0, SECTORS)
        def _(k):
            out[k] = mid[kb_ref[k]]

        for s in range(1, CHIPS):
            for t in range(2):
                second(which, s, t, True).start()
        for t in range(2):
            @pl.when(core == t)
            def _():
                second(which, 0, t, False).start()

            @pl.when(core != t)
            def _():
                second(which, 0, t, True).start()

    for g in range(GROUPS):
        r_in(g).wait()
        parts = [jnp.dot(order, r_v[g * GROUP + i], preferred_element_type=F32).astype(BF16) for i in range(GROUP)]
        packed = jnp.concatenate(parts, axis=1)
        send0[:, g * GL:(g + 1) * GL] = packed[:N0]
        send1[g // 2, :, (g % 2) * GL:(g % 2 + 1) * GL] = packed[N0:]
        if g == 0:
            pl.semaphore_wait(barrier, SECTORS - 1 + 6)
        if g < 2:
            start_first(g)
    for unit in (GROUPS, GROUPS + 1, 2, 3):
        start_first(unit)

    pair_row = jnp.concatenate(
        [jnp.full((1, V), occ_ref[pair_ref[0, p]] + occ_ref[pair_ref[1, p]], F32) for p in range(PAIRS)], axis=1
    )
    own_vir = own_vir_ref[pl.ds(me, 1), :]
    own_row = jnp.concatenate([own_vir] * PAIRS, axis=1)
    for r in range(R0 + R1):
        den[r:r + 1, :] = (pair_row - vir_ref[kb_ref[me], (R0 + R1) * vert + r]) - own_row

    t_in.wait()
    for q in range(PAIRS // QP):
        t_cat[q] = jnp.concatenate([t_v[q * QP + i] for i in range(QP)], axis=1)

    @pl.loop(0, GROUPS)
    def _(g):
        l_in(g).wait()

        @pl.loop(0, PAIRS // QP)
        def _(q):
            amps = t_cat[q]
            outs = []
            for i in range(GROUP):
                rows = pl.ds(pl.multiple_of(g * GL + i * V, 16), V)
                outs.append(jnp.dot(l_v[rows, :], amps, preferred_element_type=F32).astype(BF16))
            for i in range(QP):
                rows = pl.ds(pl.multiple_of(q * QP * V + i * V, 16), V)
                h[rows, pl.ds(pl.multiple_of(g * GL, 128), GL)] = jnp.concatenate(
                    [o[:, i * V:(i + 1) * V] for o in outs], axis=1
                )

        @pl.when(g == GROUPS // 2 - 1)
        def _():
            start_second(0)

        @pl.when(g == GROUPS // 2)
        def _():
            start_second(2)

    start_second(1)

    def arrive(half):
        for g in range(2):
            part = recv.at[half, pl.ds(0, N0), pl.ds(g * GL, GL)]
            pltpu.make_async_copy(part, part, qr_sem.at[2 * half + g]).wait()
        part = recv.at[half, pl.ds(N0, N1), :]
        pltpu.make_async_copy(part, part, qr_sem.at[GROUPS + half]).wait()

    def product(rows, half):
        return lax.dot_general(
            h[rows, half * 2 * GL:(half + 1) * 2 * GL], recv[half, :, :2 * GL], (((1,), (1,)), ((), ())),
            preferred_element_type=F32,
        )

    def y_copy(part, s):
        return pltpu.make_async_remote_copy(
            src_ref=ysend.at[part, lax.rem(y + s, 4), :, pl.ds(0, WIDE[part])],
            dst_ref=yrecv.at[part, s - 1, :, pl.ds(0, WIDE[part])],
            send_sem=ys_sem.at[part, s - 1], recv_sem=yr_sem.at[part, s - 1],
            device_id=y_peers[s - 1], device_id_type=MESH,
        )

    def z_copy(part, s):
        return pltpu.make_async_remote_copy(
            src_ref=zsend.at[part, lax.rem(z + s, 4), :, pl.ds(0, WIDE[part])],
            dst_ref=zrecv.at[part, s - 1, :, pl.ds(0, WIDE[part])],
            send_sem=zs_sem.at[part, s - 1], recv_sem=zr_sem.at[part, s - 1],
            device_id=z_peers[s - 1], device_id_type=MESH,
        )

    def y_send(part):
        @pl.loop(0, WIDE[part] // 128)
        def _(m):
            at = pl.ds(pl.multiple_of(m * 128, 128), 128)
            rows = pl.ds(pl.multiple_of(FROM[part] + m * 128, 128), 128)
            early, late = acc[rows, :N0].T, acc[rows, N0:].T
            for j in range(4):
                full[part, j, 0:32, at] = early[32 * j:32 * (j + 1)]
                full[part, j, 32:44, at] = late[12 * j:12 * (j + 1)]
        for j in range(4):
            ysend[part, j] = full[part, j].astype(BF16)
        for s in (1, 2, 3):
            y_copy(part, s).start()

    def z_send(part):
        w = WIDE[part]
        for s in (1, 2, 3):
            y_copy(part, s).wait()
        total = full[part, y, :, :w]
        for s in range(3):
            total = total + yrecv[part, s, :, :w].astype(F32)
        for j in range(4):
            zsum[part, j, 0:8, :w] = total[8 * j:8 * j + 8]
            zsum[part, j, 8:11, :w] = total[32 + 3 * j:35 + 3 * j]
        for j in range(4):
            zsend[part, j] = zsum[part, j].astype(BF16)
        for s in (1, 2, 3):
            z_copy(part, s).start()

    def finish(part):
        w, at = WIDE[part], FROM[part]
        for s in (1, 2, 3):
            z_copy(part, s).wait()
        total = zsum[part, z, :, :w]
        for s in range(3):
            total = total + zrecv[part, s, :, :w].astype(F32)
        o_ref[:, at:at + w] = total[:R0 + R1] / den[:R0 + R1, at:at + w]

    full[...] = jnp.zeros_like(full)
    zsum[...] = jnp.zeros_like(zsum)

    arrive(0)

    @pl.loop(0, 4)
    def _(m):
        rows = pl.ds(pl.multiple_of(m * (PA // 4), 16), PA // 4)
        acc[rows, :] = product(rows, 0)

    arrive(1)
    for part in range(4):
        @pl.loop(0, 2)
        def _(m):
            rows = pl.ds(pl.multiple_of(FROM[part] + m * (WIDE[part] // 2), 64), WIDE[part] // 2)
            acc[rows, :] += product(rows, 1)

        y_send(part)
        if part == 2:
            z_send(0)
    for part in (1, 2, 3):
        z_send(part)
        finish(part - 1)
    finish(3)

    for unit in range(GROUPS + 2):
        @pl.when(core != unit % 2)
        def _():
            first(unit, 0, True).wait_send()

        for s in range(1, CHIPS):
            first(unit, s, True).wait_send()
    for which in range(3):
        for t in range(2):
            @pl.when(core != t)
            def _():
                second(which, 0, t, True).wait_send()

            for s in range(1, CHIPS):
                second(which, s, t, True).wait_send()


def update_of(kb_table, pair_list, occ_energy, vir_energy, left, right, amps):
    any_space = pl.BlockSpec(memory_space=pl.ANY)
    smem = pl.BlockSpec(memory_space=pltpu.SMEM)
    vmem = pltpu.VMEM
    return pl.pallas_call(
        kernel,
        out_shape=jax.ShapeDtypeStruct((R0 + R1, PA), F32),
        in_specs=[smem] * 4 + [pl.BlockSpec(memory_space=pltpu.VMEM)] + [any_space] * 3,
        out_specs=pl.BlockSpec(memory_space=pltpu.VMEM),
        scratch_shapes=[
            vmem((KL, V), BF16), vmem((AUX, V, V), BF16), vmem((PAIRS, V, V), BF16),
            vmem((PAIRS // QP, V, QP * V), BF16),
            vmem((N0, KL), BF16), vmem((2, N1, W1 * CHIPS), BF16),
            vmem((SECTORS, 16, GL), BF16), vmem((SECTORS, 16, GL), BF16), vmem((SECTORS, N1, W1), BF16),
            vmem((2, SECTORS, 16, GL), BF16), vmem((SECTORS, N1, W1), BF16),
            vmem((2, V, W1 * CHIPS), BF16), vmem((PA, KL), BF16), vmem((PA, V), F32), vmem((16, PA), F32),
            vmem((4, 4, 48, 896), F32), vmem((4, 4, 48, 896), BF16), vmem((4, 3, 48, 896), BF16),
            vmem((4, 4, 16, 896), F32), vmem((4, 4, 16, 896), BF16), vmem((4, 3, 16, 896), BF16),
            pltpu.SemaphoreType.DMA((2 * GROUPS + 1,)),
            pltpu.SemaphoreType.DMA((GROUPS + 2, CHIPS)), pltpu.SemaphoreType.DMA((3,)),
            pltpu.SemaphoreType.DMA((3, SECTORS)), pltpu.SemaphoreType.DMA((GROUPS + 2,)),
            pltpu.SemaphoreType.DMA((4, 3)), pltpu.SemaphoreType.DMA((4, 3)),
            pltpu.SemaphoreType.DMA((4, 3)), pltpu.SemaphoreType.DMA((4, 3)),
        ],
        compiler_params=pltpu.CompilerParams(
            collective_id=0, has_side_effects=True, vmem_limit_bytes=60 * 2**20
        ),
    )(kb_table, pair_list, occ_energy, vir_energy, vir_energy, left, right, amps)


def on_device(left_factor, right_factor, amplitudes, kb_table, pair_list, occ_energy, vir_energy):
    left = left_factor.reshape(KL, V)
    right = right_factor.reshape(AUX, V, V)
    amps = amplitudes.reshape(PAIRS, V, V)
    update = update_of(kb_table, pair_list.T, occ_energy, vir_energy, left, right, amps)
    return update.reshape(1, R0 + R1, PAIRS, V)


def solution(mesh):
    placed = (
        P("ka", None, "vert", None, None),
        P("ka", None, "vert", None, None),
        P(),
        P(),
        P(),
        P(),
        P(),
    )
    return jax.shard_map(
        on_device,
        mesh=mesh,
        in_specs=placed,
        out_specs=P("ka", "vert", None, None),
        check_vma=False,
    )
```

```python
import jax
import jax.numpy as jnp
from jax import lax
from jax.experimental import pallas as pl
from jax.experimental.pallas import tpu as pltpu
from jax.sharding import PartitionSpec as P

MESH = pl.DeviceIdType.MESH
F32 = jnp.float32
BF16 = jnp.bfloat16

V = 176
AUX = 32
PAIRS = 16
SECTORS = 16
GROUP = 8
GROUPS = AUX // GROUP
GL = GROUP * V
KL = AUX * V
PA = PAIRS * V
WIDE = (512, 896, 896, 512)
FROM = (0, 512, 1408, 2304)
QP = 4
R0, R1 = 8, 3
N0, N1 = 16 * R0, 16 * R1
CHIPS = 8
W1 = 384


def kernel(kb_ref, pair_ref, occ_ref, vir_ref, own_vir_ref, l_hbm, r_hbm, t_hbm, o_ref,
           l_v, r_v, t_v, t_cat, send0, send1, mid_a, mid_b, mid_c, out0, out1, recv, h, acc, den,
           full, ysend, yrecv, zsum, zsend, zrecv,
           in_sem, ps_sem, pr_sem, qs_sem, qr_sem, ys_sem, yr_sem, zs_sem, zr_sem):
    me = lax.axis_index("ka")
    vert = lax.axis_index("vert")
    chip, core = me // 2, me % 2
    y, z = vert // 4, vert % 4
    y_peers = [(me, lax.rem(y + s, 4) * 4 + z) for s in (1, 2, 3)]
    z_peers = [(me, y * 4 + lax.rem(z + s, 4)) for s in (1, 2, 3)]

    def r_in(g):
        return pltpu.make_async_copy(r_hbm.at[pl.ds(g * GROUP, GROUP)], r_v.at[pl.ds(g * GROUP, GROUP)], in_sem.at[g])

    def l_in(g):
        rows = pl.ds(pl.multiple_of(g * GL, 16), GL)
        return pltpu.make_async_copy(l_hbm.at[rows], l_v.at[rows], in_sem.at[GROUPS + g])

    t_in = pltpu.make_async_copy(t_hbm, t_v, in_sem.at[2 * GROUPS])
    for g in range(GROUPS):
        r_in(g).start()
    t_in.start()
    for g in range(GROUPS):
        l_in(g).start()

    barrier = pltpu.get_barrier_semaphore()
    for peer in y_peers + z_peers:
        pl.semaphore_signal(barrier, inc=1, device_id=peer, device_id_type=MESH)

    @pl.loop(1, SECTORS)
    def _(s):
        pl.semaphore_signal(barrier, inc=1, device_id=(lax.rem(me + s, SECTORS), vert), device_id_type=MESH)

    mids = (mid_a, mid_b, mid_c)

    row = lax.broadcasted_iota(jnp.int32, (V, V), 0)
    col = lax.broadcasted_iota(jnp.int32, (V, V), 1)
    late = row - N0
    third = lax.shift_right_logical(late * 21846, 16)
    source = jnp.where(row < N0, 11 * lax.shift_right_logical(row, 3) + (row & 7), 11 * third + R0 + (late - 3 * third))
    order = (col == source).astype(F32).astype(BF16)

    for half in range(2):
        send1[half, :, 2 * GL:] = jnp.zeros((N1, W1 * CHIPS - 2 * GL), BF16)

    def hop(src, dst, send_sem, recv_sem, target, far):
        if far:
            return pltpu.make_async_remote_copy(
                src_ref=src, dst_ref=dst, send_sem=send_sem, recv_sem=recv_sem,
                device_id=(target, vert), device_id_type=MESH,
            )
        return pltpu.make_async_copy(src, dst, recv_sem)

    def first(unit, s, far):
        j = lax.rem(chip + s, CHIPS)
        if unit < GROUPS:
            src = send0.at[pl.ds(pl.multiple_of(16 * j, 16), 16), pl.ds(unit * GL, GL)]
            dst = mids[unit // 2].at[me]
            which = unit // 2
        else:
            src = send1.at[unit - GROUPS, :, pl.ds(pl.multiple_of(W1 * j, 128), W1)]
            dst = mids[2].at[me]
            which = 2
        return hop(src, dst, ps_sem.at[unit, s], pr_sem.at[which], 2 * j + unit % 2, far)

    def second(which, s, t, far):
        j = lax.rem(chip + s, CHIPS)
        k = 2 * j + t
        if which < 2:
            src = out0.at[which, k]
            g = 2 * which + core
            dst = recv.at[which, pl.ds(pl.multiple_of(16 * chip, 16), 16), pl.ds(pl.multiple_of(core * GL, 128), GL)]
        else:
            src = out1.at[k]
            g = GROUPS + core
            dst = recv.at[core, pl.ds(N0, N1), pl.ds(pl.multiple_of(W1 * chip, 128), W1)]
        return hop(src, dst, qs_sem.at[which, 2 * s + t], qr_sem.at[g], k, far)

    def start_first(unit):
        @pl.when(core == unit % 2)
        def _():
            first(unit, 0, False).start()

        @pl.when(core != unit % 2)
        def _():
            first(unit, 0, True).start()

        for s in range(1, CHIPS):
            first(unit, s, True).start()

    def start_second(which):
        mid, out = mids[which], out0.at[which] if which < 2 else out1
        pltpu.make_async_copy(mid, mid, pr_sem.at[which]).wait()

        @pl.loop(0, SECTORS)
        def _(k):
            out[k] = mid[kb_ref[k]]

        for s in range(1, CHIPS):
            for t in range(2):
                second(which, s, t, True).start()
        for t in range(2):
            @pl.when(core == t)
            def _():
                second(which, 0, t, False).start()

            @pl.when(core != t)
            def _():
                second(which, 0, t, True).start()

    for g in range(GROUPS):
        r_in(g).wait()
        parts = [jnp.dot(order, r_v[g * GROUP + i], preferred_element_type=F32).astype(BF16) for i in range(GROUP)]
        packed = jnp.concatenate(parts, axis=1)
        send0[:, g * GL:(g + 1) * GL] = packed[:N0]
        send1[g // 2, :, (g % 2) * GL:(g % 2 + 1) * GL] = packed[N0:]
        if g == 0:
            pl.semaphore_wait(barrier, SECTORS - 1 + 6)
        if g < 2:
            start_first(g)
    for unit in (GROUPS, GROUPS + 1, 2, 3):
        start_first(unit)

    pair_row = jnp.concatenate(
        [jnp.full((1, V), occ_ref[pair_ref[0, p]] + occ_ref[pair_ref[1, p]], F32) for p in range(PAIRS)], axis=1
    )
    own_vir = own_vir_ref[pl.ds(me, 1), :]
    own_row = jnp.concatenate([own_vir] * PAIRS, axis=1)
    for r in range(R0 + R1):
        den[r:r + 1, :] = (pair_row - vir_ref[kb_ref[me], (R0 + R1) * vert + r]) - own_row

    t_in.wait()
    for q in range(PAIRS // QP):
        t_cat[q] = jnp.concatenate([t_v[q * QP + i] for i in range(QP)], axis=1)

    @pl.loop(0, GROUPS)
    def _(g):
        l_in(g).wait()

        @pl.loop(0, PAIRS // QP)
        def _(q):
            amps = t_cat[q]
            outs = []
            for i in range(GROUP):
                rows = pl.ds(pl.multiple_of(g * GL + i * V, 16), V)
                outs.append(jnp.dot(l_v[rows, :], amps, preferred_element_type=F32).astype(BF16))
            for i in range(QP):
                rows = pl.ds(pl.multiple_of(q * QP * V + i * V, 16), V)
                h[rows, pl.ds(pl.multiple_of(g * GL, 128), GL)] = jnp.concatenate(
                    [o[:, i * V:(i + 1) * V] for o in outs], axis=1
                )

        @pl.when(g == GROUPS // 2 - 1)
        def _():
            start_second(0)

        @pl.when(g == GROUPS // 2)
        def _():
            start_second(2)

    start_second(1)

    def sent_first():
        for unit in range(GROUPS + 2):
            @pl.when(core != unit % 2)
            def _():
                first(unit, 0, True).wait_send()

            for s in range(1, CHIPS):
                first(unit, s, True).wait_send()

    def sent_second(which):
        for t in range(2):
            @pl.when(core != t)
            def _():
                second(which, 0, t, True).wait_send()

            for s in range(1, CHIPS):
                second(which, s, t, True).wait_send()

    def arrive(half):
        for g in range(2):
            part = recv.at[half, pl.ds(0, N0), pl.ds(g * GL, GL)]
            pltpu.make_async_copy(part, part, qr_sem.at[2 * half + g]).wait()
        part = recv.at[half, pl.ds(N0, N1), :]
        pltpu.make_async_copy(part, part, qr_sem.at[GROUPS + half]).wait()

    def product(rows, half):
        return lax.dot_general(
            h[rows, half * 2 * GL:(half + 1) * 2 * GL], recv[half, :, :2 * GL], (((1,), (1,)), ((), ())),
            preferred_element_type=F32,
        )

    def y_copy(part, s):
        return pltpu.make_async_remote_copy(
            src_ref=ysend.at[part, lax.rem(y + s, 4), :, pl.ds(0, WIDE[part])],
            dst_ref=yrecv.at[part, s - 1, :, pl.ds(0, WIDE[part])],
            send_sem=ys_sem.at[part, s - 1], recv_sem=yr_sem.at[part, s - 1],
            device_id=y_peers[s - 1], device_id_type=MESH,
        )

    def z_copy(part, s):
        return pltpu.make_async_remote_copy(
            src_ref=zsend.at[part, lax.rem(z + s, 4), :, pl.ds(0, WIDE[part])],
            dst_ref=zrecv.at[part, s - 1, :, pl.ds(0, WIDE[part])],
            send_sem=zs_sem.at[part, s - 1], recv_sem=zr_sem.at[part, s - 1],
            device_id=z_peers[s - 1], device_id_type=MESH,
        )

    def y_send(part):
        @pl.loop(0, WIDE[part] // 128)
        def _(m):
            at = pl.ds(pl.multiple_of(m * 128, 128), 128)
            rows = pl.ds(pl.multiple_of(FROM[part] + m * 128, 128), 128)
            early, late = acc[rows, :N0].T, acc[rows, N0:].T
            for j in range(4):
                full[part, j, 0:32, at] = early[32 * j:32 * (j + 1)]
                full[part, j, 32:44, at] = late[12 * j:12 * (j + 1)]
        for j in range(4):
            ysend[part, j] = full[part, j].astype(BF16)
        for s in (1, 2, 3):
            y_copy(part, s).start()

    def z_send(part):
        w = WIDE[part]
        for s in (1, 2, 3):
            y_copy(part, s).wait()
        total = full[part, y, :, :w]
        for s in range(3):
            total = total + yrecv[part, s, :, :w].astype(F32)
        for j in range(4):
            zsum[part, j, 0:8, :w] = total[8 * j:8 * j + 8]
            zsum[part, j, 8:11, :w] = total[32 + 3 * j:35 + 3 * j]
        for j in range(4):
            zsend[part, j] = zsum[part, j].astype(BF16)
        for s in (1, 2, 3):
            z_copy(part, s).start()

    def finish(part):
        w, at = WIDE[part], FROM[part]
        for s in (1, 2, 3):
            z_copy(part, s).wait()
        total = zsum[part, z, :, :w]
        for s in range(3):
            total = total + zrecv[part, s, :, :w].astype(F32)
        den[:R0 + R1, at:at + w] = total[:R0 + R1] / den[:R0 + R1, at:at + w]
        for p in range(PAIRS):
            if at < (p + 1) * V <= at + w:
                o_ref[:, p, :] = den[:R0 + R1, p * V:(p + 1) * V]

    full[...] = jnp.zeros_like(full)
    zsum[...] = jnp.zeros_like(zsum)

    sent_first()
    arrive(0)

    @pl.loop(0, 4)
    def _(m):
        rows = pl.ds(pl.multiple_of(m * (PA // 4), 16), PA // 4)
        acc[rows, :] = product(rows, 0)

    sent_second(0)
    sent_second(2)
    arrive(1)
    for part in range(4):
        @pl.loop(0, 2)
        def _(m):
            rows = pl.ds(pl.multiple_of(FROM[part] + m * (WIDE[part] // 2), 64), WIDE[part] // 2)
            acc[rows, :] += product(rows, 1)

        y_send(part)
        if part == 2:
            z_send(0)
    sent_second(1)
    for part in (1, 2, 3):
        z_send(part)
        finish(part - 1)
    finish(3)


def update_of(kb_table, pair_list, occ_energy, vir_energy, left, right, amps):
    any_space = pl.BlockSpec(memory_space=pl.ANY)
    smem = pl.BlockSpec(memory_space=pltpu.SMEM)
    vmem = pltpu.VMEM
    return pl.pallas_call(
        kernel,
        out_shape=jax.ShapeDtypeStruct((R0 + R1, PAIRS, V), F32),
        in_specs=[smem] * 4 + [pl.BlockSpec(memory_space=pltpu.VMEM)] + [any_space] * 3,
        out_specs=pl.BlockSpec(memory_space=pltpu.VMEM),
        scratch_shapes=[
            vmem((KL, V), BF16), vmem((AUX, V, V), BF16), vmem((PAIRS, V, V), BF16),
            vmem((PAIRS // QP, V, QP * V), BF16),
            vmem((N0, KL), BF16), vmem((2, N1, W1 * CHIPS), BF16),
            vmem((SECTORS, 16, GL), BF16), vmem((SECTORS, 16, GL), BF16), vmem((SECTORS, N1, W1), BF16),
            vmem((2, SECTORS, 16, GL), BF16), vmem((SECTORS, N1, W1), BF16),
            vmem((2, V, W1 * CHIPS), BF16), vmem((PA, KL), BF16), vmem((PA, V), F32), vmem((16, PA), F32),
            vmem((4, 4, 48, 896), F32), vmem((4, 4, 48, 896), BF16), vmem((4, 3, 48, 896), BF16),
            vmem((4, 4, 16, 896), F32), vmem((4, 4, 16, 896), BF16), vmem((4, 3, 16, 896), BF16),
            pltpu.SemaphoreType.DMA((2 * GROUPS + 1,)),
            pltpu.SemaphoreType.DMA((GROUPS + 2, CHIPS)), pltpu.SemaphoreType.DMA((3,)),
            pltpu.SemaphoreType.DMA((3, SECTORS)), pltpu.SemaphoreType.DMA((GROUPS + 2,)),
            pltpu.SemaphoreType.DMA((4, 3)), pltpu.SemaphoreType.DMA((4, 3)),
            pltpu.SemaphoreType.DMA((4, 3)), pltpu.SemaphoreType.DMA((4, 3)),
        ],
        compiler_params=pltpu.CompilerParams(
            collective_id=0, has_side_effects=True, vmem_limit_bytes=60 * 2**20
        ),
    )(kb_table, pair_list, occ_energy, vir_energy, vir_energy, left, right, amps)


def on_device(left_factor, right_factor, amplitudes, kb_table, pair_list, occ_energy, vir_energy):
    left = left_factor.reshape(KL, V)
    right = right_factor.reshape(AUX, V, V)
    amps = amplitudes.reshape(PAIRS, V, V)
    update = update_of(kb_table, pair_list.T, occ_energy, vir_energy, left, right, amps)
    return update.reshape(1, R0 + R1, PAIRS, V)


def solution(mesh):
    placed = (
        P("ka", None, "vert", None, None),
        P("ka", None, "vert", None, None),
        P(),
        P(),
        P(),
        P(),
        P(),
    )
    return jax.shard_map(
        on_device,
        mesh=mesh,
        in_specs=placed,
        out_specs=P("ka", "vert", None, None),
        check_vma=False,
    )
```
